32 devices in a mesh: group: 2 (over x), shard: 16 (over z, y, core).
Axes of the slice: x: 2, y: 2, z: 4, core: 2. Of those that a mesh axis runs over, the one named last changes fastest.
Arguments:
- coords: float32 [2, 4096], P(None, ('group', 'shard')), may hold values from 0 to 3
- probes: float32 [256, 4096], P(None, ('group', 'shard')), may hold values from -6 to 6
- neighbours: int32 [64, 8], P(('group', 'shard')), may hold values from -1 to 62, as said below
Outputs:
- precision_probe: float32 [256, 4096], P(None, ('group', 'shard'))
- cond_logvar: float32 [64], P(('group', 'shard'))
The draws below stay inside these ranges and needn't reach their ends.
Inputs may be any that keep to these rules, and one draw needn't show every extreme that they name: neighbours[b] lists 8 different blocks earlier than b, the first one b - 1; every listed block lies on the device of block b (device b // 2 in the order of group+shard) or on one of the 15 devices before it; -1 stands for a missing block, only where fewer earlier blocks exist in that reach.
All inputs are finite; a program needn't handle non-finite values.
Results may differ from the reference program's by a relative error of at most 0.0003.
Values sent between devices are 32-bit elements; how exact they have to be, the bound alone decides.
No kernel may reach another device: no remote copies, remote signals or barrier semaphores. Data moves between devices by JAX's collectives and lax.ppermute only.
A program may use at most 64 MiB of HBM per device.

```python
import jax
import jax.numpy as jnp
from jax import lax

PTS = 64
NEIGH = 8
PROBES = 256
SPAN = 16
BLK_DEV = 2
BLOCKS = 64
POINTS = 4096


def draw_neighbours(key, part):
    block_ids = jnp.arange(BLOCKS, dtype=jnp.int32)
    reach_all = SPAN * BLK_DEV
    offsets = jnp.arange(1, reach_all + 1, dtype=jnp.int32)
    allowed = (SPAN - 1) * BLK_DEV + block_ids % BLK_DEV
    noise_vals = jax.random.randint(key, (BLOCKS, reach_all), 0, 1 << 20, dtype=jnp.int32)
    scores = noise_vals * (reach_all + 1) + offsets[None, :]
    scores = jnp.where(offsets[None, :] == 1, -1, scores)
    scores = jnp.where(offsets[None, :] > allowed[:, None], scores + (1 << 30), scores)
    ranked = jnp.argsort(scores, axis=1, stable=True)[:, :NEIGH].astype(jnp.int32)
    chosen = block_ids[:, None] - (ranked + 1)
    return jnp.where(chosen >= 0, chosen, -1).astype(jnp.int32)


def block_levels(stream_key, extent, pieces, smallest, high):
    def one(dim, blocks):
        draws = jax.random.uniform(jax.random.fold_in(jax.random.fold_in(stream_key, 6), dim), (blocks,), jnp.float32, smallest / len(pieces), high / len(pieces))
        return jnp.repeat(jnp.exp(draws), extent[dim] // blocks).reshape((-1,) + (1,) * (len(extent) - dim - 1))

    loudness = one(*pieces[0])
    for cut in pieces[1:]:
        loudness = loudness * one(*cut)
    return loudness


def gaussian(key, extent, spread, most, split=(), held_as=jnp.bfloat16):
    gain = block_levels(key, extent, split, -0.22, 0.18) if split else 1.0
    array = jax.random.normal(key, extent, jnp.float32) * spread * gain
    return jnp.minimum(jnp.maximum(array, -most), most).astype(held_as)


def setup_inputs(seed: int = 0) -> dict:
    arg_keys = jax.random.split(jax.random.key(seed), 4)
    coords = jnp.clip(3.0 * jax.random.uniform(arg_keys[0], (2, POINTS), jnp.float32) ** block_levels(arg_keys[0], (2, POINTS), ((1, 32),), -0.2, 0.2), 0.0, 3.0)
    probes = gaussian(arg_keys[1], (PROBES, POINTS), 1.0, 6.0, ((1, 32),), jnp.float32)
    neighbours = draw_neighbours(jax.random.fold_in(arg_keys[3], 71), 0)
    return {"coords": coords, "probes": probes, "neighbours": neighbours}


SQRT_THREE = 1.7320508075688772
NUGGET = 0.25

def covariance(first_coord, second_coord, valid_mask):
    delta_first = first_coord[:, None] - first_coord[None, :]
    delta_second = second_coord[:, None] - second_coord[None, :]
    scaled = SQRT_THREE * jnp.sqrt(delta_first * delta_first + delta_second * delta_second)
    kernel = (1.0 + scaled) * jnp.exp(-scaled)
    identity = jnp.eye(first_coord.shape[0], dtype=first_coord.dtype)
    return valid_mask[:, None] * valid_mask[None, :] * kernel + identity * (NUGGET * valid_mask + (1.0 - valid_mask))

def precision_terms(factor, right_side, valid_mask, cond_rows):
    forward = lax.linalg.triangular_solve(factor, right_side, left_side=True, lower=True)
    keeper = (jnp.arange(right_side.shape[0]) >= cond_rows).astype(right_side.dtype)
    whitened = forward * keeper[:, None]
    backward = lax.linalg.triangular_solve(factor, whitened, left_side=True, lower=True, transpose_a=True)
    return backward * valid_mask[:, None]

def log_variance(factor, cond_rows):
    diagonal = jnp.diagonal(factor)[cond_rows:]
    return 2.0 * jnp.mean(jnp.log(diagonal))

def reference(coords, probes, neighbours):
    probe_rows = probes.T
    within = jnp.arange(PTS, dtype=jnp.int32)
    cond_rows = NEIGH * PTS

    def visit_block(summed, block_id):
        listed = neighbours[block_id]
        present = listed >= 0
        members = jnp.concatenate([jnp.where(present, listed, 0), block_id[None]]).astype(jnp.int32)
        member_ok = jnp.concatenate([present, jnp.ones((1,), dtype=bool)])
        point_ids = (members[:, None] * PTS + within[None, :]).reshape(-1)
        valid_mask = jnp.repeat(member_ok, PTS).astype(coords.dtype)
        first_coord = coords[0][point_ids]
        second_coord = coords[1][point_ids]
        right_side = probe_rows[point_ids] * valid_mask[:, None]
        factor = jnp.linalg.cholesky(covariance(first_coord, second_coord, valid_mask))
        backward = precision_terms(factor, right_side, valid_mask, cond_rows)
        summed = summed.at[point_ids].add(backward)
        return (summed, log_variance(factor, cond_rows))
    initial = jnp.zeros((POINTS, PROBES), dtype=coords.dtype)
    summed, log_vars = lax.scan(visit_block, initial, jnp.arange(BLOCKS, dtype=jnp.int32))
    return (summed.T, log_vars)
```

```python
import functools

import jax
import jax.numpy as jnp
from jax import lax
from jax.experimental import pallas as pl
from jax.experimental.pallas import tpu as pltpu
from jax.sharding import PartitionSpec as P

PTS = 64
NEIGH = 8
SPAN = 16
BLK = 2
CORES = 2
WIDE = 128
SQRT_THREE = 1.7320508075688772
NUGGET = 0.25
AXES = ("group", "shard")
CHIPS_BACK = SPAN // CORES
CHIP_PTS = CORES * BLK * PTS
COND = NEIGH * PTS
STEPS = COND // WIDE
HIGHEST = lax.Precision.HIGHEST
F32 = jnp.float32


def dot(a, b, dims=((1,), (0,))):
    return lax.dot_general(a, b, (dims, ((), ())), precision=HIGHEST, preferred_element_type=F32)


def iota(shape, dim):
    return lax.broadcasted_iota(jnp.int32, shape, dim)


def eye(n):
    return (iota((n, n), 0) == iota((n, n), 1)).astype(F32)


def schedule(low, high):
    rho = (high - low) / (high + low)
    factors = []
    while rho > 3e-4:
        factors.append(2.0 / (2.0 - rho * rho))
        rho = rho * rho / (2.0 - rho * rho)
    return 2.0 / (low + high), factors


def inverses(mats):
    n = mats[0].shape[0]
    alpha, factors = schedule(0.245, n + 0.26)
    ident = eye(n)
    rs = [ident - alpha * m for m in mats]
    c = factors[0]
    xs = [(alpha * c) * (ident + r) for r in rs]
    rs = [(1.0 - c) * ident + c * dot(r, r) for r in rs]
    for c in factors[1:-1]:
        nxt = [c * (x + dot(x, r)) for x, r in zip(xs, rs)]
        rs = [(1.0 - c) * ident + c * dot(r, r) for r in rs]
        xs = nxt
    c = factors[-1]
    xs = [c * (x + dot(x, r)) for x, r in zip(xs, rs)]
    es = [ident - dot(m, x) for m, x in zip(mats, xs)]
    return [x + dot(x, e) for x, e in zip(xs, es)]


def kernel_value(dx, dy):
    s = SQRT_THREE * jnp.sqrt(dx * dx + dy * dy)
    return (1.0 + s) * jnp.exp(-s)


def factor_kernel(where_ref, nb_ref, coords_ref, g_ref, s_ref):
    me = where_ref[0]
    lane = iota((1, WIDE), 1)
    low = lane < PTS

    def half_row(dev, half, coord, to_low):
        row = coords_ref[dev, pl.ds(coord, 1), :]
        swapped = pltpu.roll(row, PTS, 1)
        take = half if to_low else 1 - half
        return jnp.where(take == 1, swapped, row)

    def column(row):
        return jnp.transpose(jnp.broadcast_to(row, (WIDE, WIDE)))

    mats = []
    for b in range(BLK):
        rows, valid = [], []
        for k in range(STEPS):
            pieces, oks = [], []
            for h in range(2):
                ident = nb_ref[b, 2 * k + h]
                ok = ident >= 0
                safe = jnp.where(ok, ident, me * BLK)
                dev, half = lax.div(safe, BLK), lax.rem(safe, BLK)
                pieces.append([half_row(dev, half, c, h == 0) for c in range(2)])
                oks.append(jnp.where(ok, 1.0, 0.0).astype(F32))
            rows.append([jnp.where(low, pieces[0][c], pieces[1][c]) for c in range(2)])
            valid.append(jnp.where(low, oks[0], oks[1]))
        own = [half_row(me, b, c, True) for c in range(2)]
        cols = [[column(r) for r in row] for row in rows]
        own_cols = [column(r)[:PTS, :PTS] for r in own]
        valid_cols = [column(v) for v in valid]
        mat = {}
        for i in range(STEPS):
            for j in range(i, STEPS):
                value = kernel_value(cols[i][0] - rows[j][0], cols[i][1] - rows[j][1])
                value = valid_cols[i] * valid[j] * value
                if i == j:
                    value = value + eye(WIDE) * (NUGGET * valid[j] + (1.0 - valid[j]))
                mat[i, j] = value
            value = kernel_value(cols[i][0][:, :PTS] - own[0][:, :PTS], cols[i][1][:, :PTS] - own[1][:, :PTS])
            mat[i, STEPS] = valid_cols[i][:, :PTS] * value
        value = kernel_value(own_cols[0] - own[0][:, :PTS], own_cols[1] - own[1][:, :PTS])
        mat[STEPS, STEPS] = value + NUGGET * eye(PTS)
        mats.append(mat)
    panels = [{} for _ in range(BLK)]
    for k in range(STEPS):
        invs = inverses([m[k, k] for m in mats])
        for j in range(k + 1, STEPS + 1):
            for b in range(BLK):
                panels[b][k, j] = dot(invs[b], mats[b][k, j])
        for i in range(k + 1, STEPS + 1):
            for j in range(i, STEPS + 1):
                for b in range(BLK):
                    mats[b][i, j] = mats[b][i, j] - dot(mats[b][k, i], panels[b][k, j], ((0,), (0,)))
    solved = [{} for _ in range(BLK)]
    for k in reversed(range(STEPS)):
        for b in range(BLK):
            total = panels[b][k, STEPS]
            for j in range(k + 1, STEPS):
                total = total - dot(panels[b][k, j], solved[b][j])
            solved[b][k] = total
    schur = [m[STEPS, STEPS] for m in mats]
    schur_inv = inverses(schur)
    for k in range(STEPS):
        g_ref[k * WIDE : (k + 1) * WIDE, :] = -jnp.concatenate([s[k] for s in solved], axis=1)
    g_ref[COND : COND + PTS, :] = jnp.concatenate(schur_inv, axis=1)
    s_ref[...] = jnp.concatenate(schur, axis=1)


def apply_kernel(where_ref, nb_ref, other_ref, g_ref, h_ref, window_ref, *rest):
    outs, dense = rest[:-1], rest[-1]
    me = where_ref[0]
    chip = lax.div(me, CORES)
    dense[...] = jnp.zeros_like(dense)
    for side, (ids, src) in enumerate(((nb_ref, g_ref), (other_ref, h_ref))):
        core = lax.rem(me, CORES)
        core = core if side == 0 else 1 - core
        for b in range(BLK):
            from_lanes = slice(b * PTS, (b + 1) * PTS)
            lanes = slice((side * BLK + b) * PTS, (side * BLK + b + 1) * PTS)
            for m in range(NEIGH):
                ident = ids[b, m]

                @pl.when(ident >= 0)
                def _():
                    dev = lax.div(ident, BLK)
                    back = chip - lax.div(dev, CORES)
                    inside = lax.rem(ident, CORES * BLK)
                    row = pl.multiple_of(back * CHIP_PTS + inside * PTS, PTS)
                    dense[pl.ds(row, PTS), lanes] = src[m * PTS : (m + 1) * PTS, from_lanes]

            row = pl.multiple_of((core * BLK + b) * PTS, PTS)
            dense[pl.ds(row, PTS), lanes] = eye(PTS)
    total = None
    for o in range(CHIPS_BACK + 1):
        part = dot(window_ref[o], dense[o * CHIP_PTS : (o + 1) * CHIP_PTS, :])
        total = part if total is None else total + part
    pieces = []
    for side, src in enumerate((g_ref, h_ref)):
        for b in range(BLK):
            q = side * BLK + b
            pieces.append(dot(total[:, q * PTS : (q + 1) * PTS], src[COND : COND + PTS, b * PTS : (b + 1) * PTS]))
    scaled = jnp.concatenate(pieces, axis=1)
    for o in range(CHIPS_BACK + 1):
        outs[o][...] = dot(scaled, dense[o * CHIP_PTS : (o + 1) * CHIP_PTS, :], ((1,), (1,)))


def logdet_kernel(s_ref, out_ref, work):
    work[...] = s_ref[...]
    rows = iota((PTS, WIDE), 0)
    lanes = iota((PTS, WIDE), 1)

    def step(k, total):
        mat = work[...]
        row = work[pl.ds(k, 1), :]
        first = jnp.sum(jnp.where(lanes == k, mat, 0.0), axis=1, keepdims=True)
        second = jnp.sum(jnp.where(lanes == k + PTS, mat, 0.0), axis=1, keepdims=True)
        col = jnp.where(lanes < PTS, first, second)
        pivot = jnp.sum(jnp.where(rows == k, col, 0.0), axis=0, keepdims=True)
        work[...] = mat - col * (row / pivot)
        return total + jnp.log(pivot)

    total = lax.fori_loop(0, PTS, step, jnp.zeros((1, WIDE), F32))
    out_ref[...] = jnp.broadcast_to(total * (1.0 / PTS), out_ref.shape)


def passed(value, by):
    size = lax.axis_size(AXES)
    return lax.ppermute(value, AXES, [(i, i + by) for i in range(size) if 0 <= i + by < size])


def swapped(value):
    size = lax.axis_size(AXES)
    return lax.ppermute(value, AXES, [(i, i ^ 1) for i in range(size)])


def shards(coords, probes, neighbours):
    count = lax.axis_size(AXES)
    half = probes.shape[0] // CORES
    device = lax.axis_index(AXES)
    core = device % CORES
    here = jnp.reshape(device, (1,)).astype(jnp.int32)
    smem = pl.BlockSpec(memory_space=pltpu.SMEM)
    vmem = pl.BlockSpec(memory_space=pltpu.VMEM)

    everywhere = lax.all_to_all(
        jnp.broadcast_to(jnp.pad(coords, ((0, 6), (0, 0)))[None], (count, 8, WIDE)), AXES, 0, 0
    )
    other_neighbours = swapped(neighbours)
    kept = lax.dynamic_slice_in_dim(probes, core * half, half, 0)
    given = swapped(lax.dynamic_slice_in_dim(probes, (1 - core) * half, half, 0))
    chip_probes = jnp.where(
        core == 0, jnp.concatenate([kept, given], axis=1), jnp.concatenate([given, kept], axis=1)
    )
    window = jnp.stack([chip_probes] + [passed(chip_probes, CORES * o) for o in range(1, CHIPS_BACK + 1)])

    g, schur = pl.pallas_call(
        factor_kernel,
        out_shape=(
            jax.ShapeDtypeStruct((COND + PTS, WIDE), F32),
            jax.ShapeDtypeStruct((PTS, WIDE), F32),
        ),
        in_specs=[smem, smem, vmem],
        out_specs=(vmem, vmem),
        compiler_params=pltpu.CompilerParams(vmem_limit_bytes=32 * 2**20),
        cost_estimate=pl.CostEstimate(flops=10**9, bytes_accessed=10**6, transcendentals=10**6),
        name="factor",
    )(here, neighbours, everywhere)
    h = swapped(g)
    tile = jax.ShapeDtypeStruct((half, CHIP_PTS), F32)
    terms = pl.pallas_call(
        apply_kernel,
        out_shape=(tile,) * (CHIPS_BACK + 1),
        in_specs=[smem, smem, smem, vmem, vmem, vmem],
        out_specs=(vmem,) * (CHIPS_BACK + 1),
        scratch_shapes=[pltpu.VMEM(((CHIPS_BACK + 1) * CHIP_PTS, CORES * BLK * PTS), F32)],
        compiler_params=pltpu.CompilerParams(vmem_limit_bytes=32 * 2**20),
        cost_estimate=pl.CostEstimate(flops=10**9, bytes_accessed=10**6, transcendentals=0),
        name="apply",
    )(here, neighbours, other_neighbours, g, h, window)
    logs = pl.pallas_call(
        logdet_kernel,
        out_shape=jax.ShapeDtypeStruct((8, WIDE), F32),
        in_specs=[vmem],
        out_specs=vmem,
        scratch_shapes=[pltpu.VMEM((PTS, WIDE), F32)],
        cost_estimate=pl.CostEstimate(flops=10**7, bytes_accessed=10**6, transcendentals=0),
        name="logdet",
    )(schur)
    total = terms[0]
    for o in range(1, CHIPS_BACK + 1):
        total = total + passed(terms[o], -CORES * o)
    width = BLK * PTS
    mine = lax.dynamic_slice_in_dim(total, core * width, width, 1)
    theirs = swapped(lax.dynamic_slice_in_dim(total, (1 - core) * width, width, 1))
    result = jnp.where(
        core == 0, jnp.concatenate([mine, theirs], axis=0), jnp.concatenate([theirs, mine], axis=0)
    )
    return result, logs[0, :: PTS]


def solution(mesh):
    return jax.shard_map(
        shards,
        mesh=mesh,
        in_specs=(P(None, AXES), P(None, AXES), P(AXES, None)),
        out_specs=(P(None, AXES), P(AXES)),
        check_vma=False,
    )
```

```python
import functools

import jax
import jax.numpy as jnp
from jax import lax
from jax.experimental import pallas as pl
from jax.experimental.pallas import tpu as pltpu
from jax.sharding import PartitionSpec as P

PTS = 64
NEIGH = 8
SPAN = 16
BLK = 2
WIDE = 128
SQRT_THREE = 1.7320508075688772
NUGGET = 0.25
AXES = ("group", "shard")
SLAB = 4
WINDOW = SPAN // SLAB + 1
COND = NEIGH * PTS
STEPS = COND // WIDE
HIGHEST = lax.Precision.HIGHEST
F32 = jnp.float32


def dot(a, b, dims=((1,), (0,))):
    return lax.dot_general(a, b, (dims, ((), ())), precision=HIGHEST, preferred_element_type=F32)


def iota(shape, dim):
    return lax.broadcasted_iota(jnp.int32, shape, dim)


def eye(n):
    return (iota((n, n), 0) == iota((n, n), 1)).astype(F32)


def schedule(low, high):
    rho = (high - low) / (high + low)
    factors = []
    while rho > 3e-4:
        factors.append(2.0 / (2.0 - rho * rho))
        rho = rho * rho / (2.0 - rho * rho)
    return 2.0 / (low + high), factors


def inverses(mats):
    n = mats[0].shape[0]
    alpha, factors = schedule(0.245, n + 0.26)
    ident = eye(n)
    rs = [ident - alpha * m for m in mats]
    c = factors[0]
    xs = [(alpha * c) * (ident + r) for r in rs]
    rs = [(1.0 - c) * ident + c * dot(r, r) for r in rs]
    for c in factors[1:-1]:
        nxt = [c * (x + dot(x, r)) for x, r in zip(xs, rs)]
        rs = [(1.0 - c) * ident + c * dot(r, r) for r in rs]
        xs = nxt
    c = factors[-1]
    xs = [c * (x + dot(x, r)) for x, r in zip(xs, rs)]
    es = [ident - dot(m, x) for m, x in zip(mats, xs)]
    return [x + dot(x, e) for x, e in zip(xs, es)]


def kernel_value(dx, dy):
    s = SQRT_THREE * jnp.sqrt(dx * dx + dy * dy)
    return (1.0 + s) * jnp.exp(-s)


def factor_kernel(where_ref, nb_ref, coords_ref, g_ref, s_ref):
    me = where_ref[0]
    lane = iota((1, WIDE), 1)
    low = lane < PTS

    def half_row(dev, half, coord, to_low):
        row = coords_ref[dev, pl.ds(coord, 1), :]
        swapped = pltpu.roll(row, PTS, 1)
        take = half if to_low else 1 - half
        return jnp.where(take == 1, swapped, row)

    def column(row):
        return jnp.transpose(jnp.broadcast_to(row, (WIDE, WIDE)))

    mats = []
    for b in range(BLK):
        rows, valid = [], []
        for k in range(STEPS):
            pieces, oks = [], []
            for h in range(2):
                ident = nb_ref[b, 2 * k + h]
                ok = ident >= 0
                safe = jnp.where(ok, ident, me * BLK)
                dev, half = lax.div(safe, BLK), lax.rem(safe, BLK)
                pieces.append([half_row(dev, half, c, h == 0) for c in range(2)])
                oks.append(jnp.where(ok, 1.0, 0.0).astype(F32))
            rows.append([jnp.where(low, pieces[0][c], pieces[1][c]) for c in range(2)])
            valid.append(jnp.where(low, oks[0], oks[1]))
        own = [half_row(me, b, c, True) for c in range(2)]
        cols = [[column(r) for r in row] for row in rows]
        own_cols = [column(r)[:PTS, :PTS] for r in own]
        valid_cols = [column(v) for v in valid]
        mat = {}
        for i in range(STEPS):
            for j in range(i, STEPS):
                value = kernel_value(cols[i][0] - rows[j][0], cols[i][1] - rows[j][1])
                value = valid_cols[i] * valid[j] * value
                if i == j:
                    value = value + eye(WIDE) * (NUGGET * valid[j] + (1.0 - valid[j]))
                mat[i, j] = value
            value = kernel_value(cols[i][0][:, :PTS] - own[0][:, :PTS], cols[i][1][:, :PTS] - own[1][:, :PTS])
            mat[i, STEPS] = valid_cols[i][:, :PTS] * value
        value = kernel_value(own_cols[0] - own[0][:, :PTS], own_cols[1] - own[1][:, :PTS])
        mat[STEPS, STEPS] = value + NUGGET * eye(PTS)
        mats.append(mat)
    panels = [{} for _ in range(BLK)]
    for k in range(STEPS):
        invs = inverses([m[k, k] for m in mats])
        for j in range(k + 1, STEPS + 1):
            for b in range(BLK):
                panels[b][k, j] = dot(invs[b], mats[b][k, j])
        for i in range(k + 1, STEPS + 1):
            for j in range(i, STEPS + 1):
                for b in range(BLK):
                    mats[b][i, j] = mats[b][i, j] - dot(mats[b][k, i], panels[b][k, j], ((0,), (0,)))
    solved = [{} for _ in range(BLK)]
    for k in reversed(range(STEPS)):
        for b in range(BLK):
            total = panels[b][k, STEPS]
            for j in range(k + 1, STEPS):
                total = total - dot(panels[b][k, j], solved[b][j])
            solved[b][k] = total
    schur = [m[STEPS, STEPS] for m in mats]
    for k in range(STEPS):
        g_ref[k * WIDE : (k + 1) * WIDE, :] = -jnp.concatenate([s[k] for s in solved], axis=1)
    s_ref[...] = jnp.concatenate(schur, axis=1)


def apply_kernel(where_ref, ids_ref, *rest):
    windows, w_refs, v_refs, outs = rest[:WINDOW], rest[WINDOW : WINDOW + SLAB], rest[WINDOW + SLAB : WINDOW + 2 * SLAB], rest[WINDOW + 2 * SLAB : -2]
    held, total = rest[-2], rest[-1]
    me = where_ref[0]
    slab, quarter = lax.div(me, SLAB), lax.rem(me, SLAB)
    low = iota((PTS, WIDE), 1) < PTS
    for o in range(WINDOW):
        held[o * SLAB : (o + 1) * SLAB] = windows[o][...]
    total[...] = jnp.zeros_like(total)

    for k in range(SLAB):
        sender = quarter ^ k
        device = slab * SLAB + sender
        places = []
        for b in range(BLK):
            for m in range(NEIGH):
                ident = ids_ref[sender, b * NEIGH + m]
                ident = jnp.where(ident >= 0, ident, device * BLK)
                owner = lax.div(ident, BLK)
                place = (slab - lax.div(owner, SLAB)) * SLAB + lax.rem(owner, SLAB)
                turn = (lax.rem(ident, BLK) ^ (m % 2)) * PTS
                places.append((place, turn))
        gathered = []
        for b in range(BLK):
            pieces = []
            for m in range(0, NEIGH, 2):
                (p0, t0), (p1, t1) = places[b * NEIGH + m], places[b * NEIGH + m + 1]
                first = pltpu.roll(held[p0], t0, 1)
                second = pltpu.roll(held[p1], t1, 1)
                pieces.append(jnp.where(low, first, second))
            gathered.append(jnp.concatenate(pieces, axis=1))
        w = w_refs[k][...]
        white = dot(jnp.concatenate(gathered, axis=0), w)
        white = held[sender] + jnp.where(low, white[:PTS], white[PTS:])
        v = v_refs[k][...]
        inv = jnp.concatenate([jnp.where(low, v, 0.0), jnp.where(low, 0.0, v)], axis=0)
        scaled = dot(white, inv)
        total[sender] += scaled
        sides = jnp.concatenate([jnp.where(low, scaled, 0.0), jnp.where(low, 0.0, scaled)], axis=0)
        back = dot(sides, w, ((1,), (1,)))
        for b in range(BLK):
            for m in range(NEIGH):
                place, turn = places[b * NEIGH + m]
                tile = back[b * PTS : (b + 1) * PTS, (m // 2) * WIDE : (m // 2 + 1) * WIDE]
                tile = jnp.where(low, tile, 0.0) if m % 2 == 0 else jnp.where(low, 0.0, tile)
                total[place] += pltpu.roll(tile, turn, 1)
    for o in range(WINDOW):
        outs[o][...] = total[o * SLAB : (o + 1) * SLAB]


def invert_kernel(s_ref, v_ref):
    v_ref[...] = jnp.concatenate(inverses([s_ref[:, b * PTS : (b + 1) * PTS] for b in range(BLK)]), axis=1)


def logdet_kernel(s_ref, out_ref, work):
    work[...] = s_ref[...]
    rows = iota((PTS, WIDE), 0)
    lanes = iota((PTS, WIDE), 1)

    def step(k, total):
        mat = work[...]
        row = work[pl.ds(k, 1), :]
        first = jnp.sum(jnp.where(lanes == k, mat, 0.0), axis=1, keepdims=True)
        second = jnp.sum(jnp.where(lanes == k + PTS, mat, 0.0), axis=1, keepdims=True)
        col = jnp.where(lanes < PTS, first, second)
        pivot = jnp.sum(jnp.where(rows == k, col, 0.0), axis=0, keepdims=True)
        work[...] = mat - col * (row / pivot)
        return total + jnp.log(pivot)

    total = lax.fori_loop(0, PTS, step, jnp.zeros((1, WIDE), F32))
    out_ref[...] = jnp.broadcast_to(total * (1.0 / PTS), out_ref.shape)


def passed(value, by):
    size = lax.axis_size(AXES)
    return lax.ppermute(value, AXES, [(i, i + by) for i in range(size) if 0 <= i + by < size])


def swapped(value, mask):
    size = lax.axis_size(AXES)
    return lax.ppermute(value, AXES, [(i, i ^ mask) for i in range(size)])


def within_slab(value):
    groups = [[SLAB * j + i for i in range(SLAB)] for j in range(lax.axis_size(AXES[1]) // SLAB)]
    return lax.all_to_all(value, AXES[1], 0, 0, axis_index_groups=groups)


def shards(coords, probes, neighbours):
    count = lax.axis_size(AXES)
    quarter = probes.shape[0] // SLAB
    device = lax.axis_index(AXES)
    here = jnp.reshape(device, (1,)).astype(jnp.int32)
    smem = pl.BlockSpec(memory_space=pltpu.SMEM)
    vmem = pl.BlockSpec(memory_space=pltpu.VMEM)

    ids_row = jnp.pad(neighbours.astype(F32).reshape(1, -1), ((0, 0), (0, WIDE - BLK * NEIGH)))
    told = jnp.pad(jnp.concatenate([coords, ids_row], axis=0), ((0, 5), (0, 0)))
    everywhere = lax.all_to_all(jnp.broadcast_to(told[None], (count, 8, WIDE)), AXES, 0, 0)
    ids = lax.dynamic_slice(everywhere, (device // SLAB * SLAB, 2, 0), (SLAB, 1, BLK * NEIGH))
    ids = ids.reshape(SLAB, BLK * NEIGH).astype(jnp.int32)
    own = within_slab(probes.reshape(SLAB, quarter, WIDE))
    window = [own] + [passed(own, SLAB * o) for o in range(1, WINDOW)]

    w, schur = pl.pallas_call(
        factor_kernel,
        out_shape=(jax.ShapeDtypeStruct((COND, WIDE), F32), jax.ShapeDtypeStruct((PTS, WIDE), F32)),
        in_specs=[smem, smem, vmem],
        out_specs=(vmem, vmem),
        compiler_params=pltpu.CompilerParams(vmem_limit_bytes=32 * 2**20),
        cost_estimate=pl.CostEstimate(flops=10**9, bytes_accessed=10**6, transcendentals=10**6),
        name="factor",
    )(here, neighbours, everywhere)
    w_y = swapped(w, 2)
    w_d = swapped(w, 1)
    v = pl.pallas_call(
        invert_kernel,
        out_shape=jax.ShapeDtypeStruct((PTS, WIDE), F32),
        in_specs=[vmem],
        out_specs=vmem,
        cost_estimate=pl.CostEstimate(flops=10**8, bytes_accessed=10**5, transcendentals=0),
        name="invert",
    )(schur)
    v_y = swapped(v, 2)
    v_d = swapped(v, 1)
    w_yd = swapped(w_y, 1)
    v_yd = swapped(v_y, 1)
    tile = jax.ShapeDtypeStruct((SLAB, quarter, WIDE), F32)
    terms = pl.pallas_call(
        apply_kernel,
        out_shape=(tile,) * WINDOW,
        in_specs=[smem, smem] + [vmem] * (WINDOW + 2 * SLAB),
        out_specs=(vmem,) * WINDOW,
        scratch_shapes=[pltpu.VMEM((WINDOW * SLAB, quarter, WIDE), F32)] * 2,
        compiler_params=pltpu.CompilerParams(vmem_limit_bytes=32 * 2**20),
        cost_estimate=pl.CostEstimate(flops=10**9, bytes_accessed=10**6, transcendentals=0),
        name="apply",
    )(here, ids, *window, w, w_d, w_y, w_yd, v, v_d, v_y, v_yd)
    logs = pl.pallas_call(
        logdet_kernel,
        out_shape=jax.ShapeDtypeStruct((8, WIDE), F32),
        in_specs=[vmem],
        out_specs=vmem,
        scratch_shapes=[pltpu.VMEM((PTS, WIDE), F32)],
        cost_estimate=pl.CostEstimate(flops=10**7, bytes_accessed=10**6, transcendentals=0),
        name="logdet",
    )(schur)
    returned = [passed(terms[o], -SLAB * o) for o in range(1, WINDOW)]
    kept, logs = lax.optimization_barrier((terms[0], logs))
    total = kept
    for part in returned:
        total = total + part
    result = within_slab(total).reshape(SLAB * quarter, WIDE)
    return result, logs[0, :: PTS]


def solution(mesh):
    return jax.shard_map(
        shards,
        mesh=mesh,
        in_specs=(P(None, AXES), P(None, AXES), P(AXES, None)),
        out_specs=(P(None, AXES), P(AXES)),
        check_vma=False,
    )
```

```python
import functools

import jax
import jax.numpy as jnp
from jax import lax
from jax.experimental import pallas as pl
from jax.experimental.pallas import tpu as pltpu
from jax.sharding import PartitionSpec as P

PTS = 64
NEIGH = 8
SPAN = 16
BLK = 2
WIDE = 128
SQRT_THREE = 1.7320508075688772
NUGGET = 0.25
AXES = ("group", "shard")
SLAB = 4
WINDOW = SPAN // SLAB + 1
COND = NEIGH * PTS
STEPS = COND // WIDE
HIGHEST = lax.Precision.HIGHEST
HIGH = lax.Precision.HIGH
F32 = jnp.float32


def dot(a, b, dims=((1,), (0,)), precision=HIGHEST):
    return lax.dot_general(a, b, (dims, ((), ())), precision=precision, preferred_element_type=F32)


def quick(a, b, dims=((1,), (0,))):
    return dot(a, b, dims, HIGH)


def iota(shape, dim):
    return lax.broadcasted_iota(jnp.int32, shape, dim)


def eye(n):
    return (iota((n, n), 0) == iota((n, n), 1)).astype(F32)


def schedule(low, high):
    rho = (high - low) / (high + low)
    factors = []
    while rho > 3e-4:
        factors.append(2.0 / (2.0 - rho * rho))
        rho = rho * rho / (2.0 - rho * rho)
    return 2.0 / (low + high), factors


def inverses(mats):
    n = mats[0].shape[0]
    alpha, factors = schedule(0.245, n + 0.26)
    ident = eye(n)
    rs = [ident - alpha * m for m in mats]
    c = factors[0]
    xs = [(alpha * c) * (ident + r) for r in rs]
    rs = [(1.0 - c) * ident + c * quick(r, r) for r in rs]
    for c in factors[1:-1]:
        nxt = [c * (x + quick(x, r)) for x, r in zip(xs, rs)]
        rs = [(1.0 - c) * ident + c * quick(r, r) for r in rs]
        xs = nxt
    c = factors[-1]
    xs = [c * (x + quick(x, r)) for x, r in zip(xs, rs)]
    es = [ident - dot(m, x) for m, x in zip(mats, xs)]
    return [x + quick(x, e) for x, e in zip(xs, es)]


def kernel_value(dx, dy):
    s = SQRT_THREE * jnp.sqrt(dx * dx + dy * dy)
    return (1.0 + s) * jnp.exp(-s)


def factor_kernel(where_ref, nb_ref, coords_ref, g_ref, s_ref):
    me = where_ref[0]
    lane = iota((1, WIDE), 1)
    low = lane < PTS

    def half_row(dev, half, coord, to_low):
        row = coords_ref[dev, pl.ds(coord, 1), :]
        swapped = pltpu.roll(row, PTS, 1)
        take = half if to_low else 1 - half
        return jnp.where(take == 1, swapped, row)

    def column(row):
        return jnp.transpose(jnp.broadcast_to(row, (WIDE, WIDE)))

    mats = []
    for b in range(BLK):
        rows, valid = [], []
        for k in range(STEPS):
            pieces, oks = [], []
            for h in range(2):
                ident = nb_ref[b, 2 * k + h]
                ok = ident >= 0
                safe = jnp.where(ok, ident, me * BLK)
                dev, half = lax.div(safe, BLK), lax.rem(safe, BLK)
                pieces.append([half_row(dev, half, c, h == 0) for c in range(2)])
                oks.append(jnp.where(ok, 1.0, 0.0).astype(F32))
            rows.append([jnp.where(low, pieces[0][c], pieces[1][c]) for c in range(2)])
            valid.append(jnp.where(low, oks[0], oks[1]))
        own = [half_row(me, b, c, True) for c in range(2)]
        cols = [[column(r) for r in row] for row in rows]
        own_cols = [column(r)[:PTS, :PTS] for r in own]
        valid_cols = [column(v) for v in valid]
        mat = {}
        for i in range(STEPS):
            for j in range(i, STEPS):
                value = kernel_value(cols[i][0] - rows[j][0], cols[i][1] - rows[j][1])
                value = valid_cols[i] * valid[j] * value
                if i == j:
                    value = value + eye(WIDE) * (NUGGET * valid[j] + (1.0 - valid[j]))
                mat[i, j] = value
            value = kernel_value(cols[i][0][:, :PTS] - own[0][:, :PTS], cols[i][1][:, :PTS] - own[1][:, :PTS])
            mat[i, STEPS] = valid_cols[i][:, :PTS] * value
        value = kernel_value(own_cols[0] - own[0][:, :PTS], own_cols[1] - own[1][:, :PTS])
        mat[STEPS, STEPS] = value + NUGGET * eye(PTS)
        mats.append(mat)
    panels = [{} for _ in range(BLK)]
    for k in range(STEPS):
        invs = inverses([m[k, k] for m in mats])
        for j in range(k + 1, STEPS + 1):
            for b in range(BLK):
                panels[b][k, j] = dot(invs[b], mats[b][k, j])
        for i in range(k + 1, STEPS + 1):
            for j in range(i, STEPS + 1):
                for b in range(BLK):
                    mats[b][i, j] = mats[b][i, j] - dot(mats[b][k, i], panels[b][k, j], ((0,), (0,)))
    solved = [{} for _ in range(BLK)]
    for k in reversed(range(STEPS)):
        for b in range(BLK):
            total = panels[b][k, STEPS]
            for j in range(k + 1, STEPS):
                total = total - dot(panels[b][k, j], solved[b][j])
            solved[b][k] = total
    schur = [m[STEPS, STEPS] for m in mats]
    for k in range(STEPS):
        g_ref[k * WIDE : (k + 1) * WIDE, :] = -jnp.concatenate([s[k] for s in solved], axis=1)
    s_ref[...] = jnp.concatenate(schur, axis=1)


def apply_kernel(where_ref, ids_ref, *rest):
    windows, w_refs, v_refs, outs = rest[:WINDOW], rest[WINDOW : WINDOW + SLAB], rest[WINDOW + SLAB : WINDOW + 2 * SLAB], rest[WINDOW + 2 * SLAB : -2]
    held, total = rest[-2], rest[-1]
    me = where_ref[0]
    slab, quarter = lax.div(me, SLAB), lax.rem(me, SLAB)
    low = iota((PTS, WIDE), 1) < PTS
    for o in range(WINDOW):
        held[o * SLAB : (o + 1) * SLAB] = windows[o][...]
    total[...] = jnp.zeros_like(total)

    for k in range(SLAB):
        sender = quarter ^ k
        device = slab * SLAB + sender
        places = []
        for b in range(BLK):
            for m in range(NEIGH):
                ident = ids_ref[sender, b, m]
                ident = jnp.where(ident >= 0, ident, device * BLK)
                owner = lax.div(ident, BLK)
                place = (slab - lax.div(owner, SLAB)) * SLAB + (lax.rem(owner, SLAB) ^ quarter)
                turn = (lax.rem(ident, BLK) ^ (m % 2)) * PTS
                places.append((place, turn))
        gathered = []
        for b in range(BLK):
            pieces = []
            for m in range(0, NEIGH, 2):
                (p0, t0), (p1, t1) = places[b * NEIGH + m], places[b * NEIGH + m + 1]
                first = pltpu.roll(held[p0], t0, 1)
                second = pltpu.roll(held[p1], t1, 1)
                pieces.append(jnp.where(low, first, second))
            gathered.append(jnp.concatenate(pieces, axis=1))
        w = w_refs[k][...]
        white = quick(jnp.concatenate(gathered, axis=0), w)
        white = held[k] + jnp.where(low, white[:PTS], white[PTS:])
        v = v_refs[k][...]
        inv = jnp.concatenate([jnp.where(low, v, 0.0), jnp.where(low, 0.0, v)], axis=0)
        scaled = dot(white, inv)
        total[k] += scaled
        sides = jnp.concatenate([jnp.where(low, scaled, 0.0), jnp.where(low, 0.0, scaled)], axis=0)
        back = quick(sides, w, ((1,), (1,)))
        for b in range(BLK):
            for m in range(NEIGH):
                place, turn = places[b * NEIGH + m]
                tile = back[b * PTS : (b + 1) * PTS, (m // 2) * WIDE : (m // 2 + 1) * WIDE]
                tile = jnp.where(low, tile, 0.0) if m % 2 == 0 else jnp.where(low, 0.0, tile)
                total[place] += pltpu.roll(tile, turn, 1)
    for o in range(WINDOW):
        outs[o][...] = total[o * SLAB : (o + 1) * SLAB]


def invert_kernel(s_ref, v_ref):
    v_ref[...] = jnp.concatenate(inverses([s_ref[:, b * PTS : (b + 1) * PTS] for b in range(BLK)]), axis=1)


def logdet_kernel(s_ref, out_ref, work):
    work[...] = s_ref[...]
    rows = iota((PTS, WIDE), 0)
    lanes = iota((PTS, WIDE), 1)

    def step(k, total):
        mat = work[...]
        row = work[pl.ds(k, 1), :]
        first = jnp.sum(jnp.where(lanes == k, mat, 0.0), axis=1, keepdims=True)
        second = jnp.sum(jnp.where(lanes == k + PTS, mat, 0.0), axis=1, keepdims=True)
        col = jnp.where(lanes < PTS, first, second)
        pivot = jnp.sum(jnp.where(rows == k, col, 0.0), axis=0, keepdims=True)
        work[...] = mat - col * (row / pivot)
        return total + jnp.log(pivot)

    total = lax.fori_loop(0, PTS, step, jnp.zeros((1, WIDE), F32))
    out_ref[...] = jnp.broadcast_to(total * (1.0 / PTS), out_ref.shape)


def prepare_kernel(where_ref, coords_ref, nb_ref, probes_ref, told_ref, *outs_and_scratch):
    outs, scratch = outs_and_scratch[:-1], outs_and_scratch[-1]
    quarter = lax.rem(where_ref[0], SLAB)
    rows = outs[0].shape[0]
    scratch[...] = jnp.zeros_like(scratch)
    scratch[:2, :] = coords_ref[...]
    scratch[2 : 2 + BLK, :NEIGH] = nb_ref[...].astype(F32)
    told_ref[...] = jnp.broadcast_to(scratch[...][None], told_ref.shape)
    for k in range(SLAB):
        outs[k][...] = probes_ref[pl.ds(pl.multiple_of((quarter ^ k) * rows, rows), rows), :]


def sum_kernel(*refs):
    terms, outs = refs[:WINDOW], refs[WINDOW:]
    for k in range(SLAB):
        value = terms[0][k]
        for o in range(1, WINDOW):
            value = value + terms[o][k]
        outs[k][...] = value


def place_kernel(where_ref, *refs):
    tiles, out_ref = refs[:SLAB], refs[SLAB]
    quarter = lax.rem(where_ref[0], SLAB)
    rows = tiles[0].shape[0]
    for k in range(SLAB):
        out_ref[pl.ds(pl.multiple_of((quarter ^ k) * rows, rows), rows), :] = tiles[k][...]


def passed(value, by):
    size = lax.axis_size(AXES)
    return lax.ppermute(value, AXES, [(i, i + by) for i in range(size) if 0 <= i + by < size])


def swapped(value, mask):
    size = lax.axis_size(AXES)
    return lax.ppermute(value, AXES, [(i, i ^ mask) for i in range(size)])


def local(kernel, name, outs, specs, scratch=(), gflops=1):
    vmem = pl.BlockSpec(memory_space=pltpu.VMEM)
    return pl.pallas_call(
        kernel,
        out_shape=outs,
        in_specs=specs,
        out_specs=jax.tree.map(lambda _: vmem, outs),
        scratch_shapes=list(scratch),
        compiler_params=pltpu.CompilerParams(vmem_limit_bytes=32 * 2**20),
        cost_estimate=pl.CostEstimate(flops=gflops * 10**9, bytes_accessed=10**5, transcendentals=0),
        name=name,
    )


def shards(coords, probes, neighbours):
    count = lax.axis_size(AXES)
    quarter = probes.shape[0] // SLAB
    device = lax.axis_index(AXES)
    here = jnp.reshape(device, (1,)).astype(jnp.int32)
    smem = pl.BlockSpec(memory_space=pltpu.SMEM)
    vmem = pl.BlockSpec(memory_space=pltpu.VMEM)
    tile = jax.ShapeDtypeStruct((quarter, WIDE), F32)
    tiles = jax.ShapeDtypeStruct((SLAB, quarter, WIDE), F32)
    square = jax.ShapeDtypeStruct((PTS, WIDE), F32)

    told, *pieces = local(
        prepare_kernel,
        "prepare",
        (jax.ShapeDtypeStruct((count, 8, WIDE), F32),) + (tile,) * SLAB,
        [smem, vmem, vmem, vmem],
        [pltpu.VMEM((8, WIDE), F32)],
    )(here, coords, neighbours, probes)
    everywhere = lax.all_to_all(told, AXES, 0, 0)
    own = jnp.stack([pieces[0]] + [swapped(pieces[k], k) for k in range(1, SLAB)])
    ids = lax.dynamic_slice(everywhere, (device // SLAB * SLAB, 2, 0), (SLAB, BLK, NEIGH)).astype(jnp.int32)
    window = [own] + [passed(own, SLAB * o) for o in range(1, WINDOW)]

    w, schur = local(
        factor_kernel,
        "factor",
        (jax.ShapeDtypeStruct((COND, WIDE), F32), square),
        [smem, smem, vmem],
        gflops=16,
    )(here, neighbours, everywhere)
    w, schur, *window = lax.optimization_barrier((w, schur, *window))
    w_y = swapped(w, 2)
    w_d = swapped(w, 1)
    v = local(invert_kernel, "invert", square, [vmem], gflops=3)(schur)
    v_d, v_y, v_yd = (swapped(v, k) for k in range(1, SLAB))
    w_y, v = lax.optimization_barrier((w_y, v))
    w_yd = swapped(w_y, 1)
    terms = local(
        apply_kernel,
        "apply",
        (tiles,) * WINDOW,
        [smem, smem] + [vmem] * (WINDOW + 2 * SLAB),
        [pltpu.VMEM((WINDOW * SLAB, quarter, WIDE), F32)] * 2,
        gflops=4,
    )(here, ids, *window, w, w_d, w_y, w_yd, v, v_d, v_y, v_yd)
    logs = local(
        logdet_kernel, "logdet", jax.ShapeDtypeStruct((8, WIDE), F32), [vmem], [pltpu.VMEM((PTS, WIDE), F32)], gflops=9
    )(schur)
    returned = [passed(terms[o], -SLAB * o) for o in range(1, WINDOW)]
    kept, logs = lax.optimization_barrier((terms[0], logs))
    sums = local(sum_kernel, "sum", (tile,) * SLAB, [vmem] * WINDOW)(kept, *returned)
    result = local(place_kernel, "place", jax.ShapeDtypeStruct(probes.shape, F32), [smem] + [vmem] * SLAB)(
        here, sums[0], *(swapped(sums[k], k) for k in range(1, SLAB))
    )
    return result, logs[0, :: PTS]


def solution(mesh):
    return jax.shard_map(
        shards,
        mesh=mesh,
        in_specs=(P(None, AXES), P(None, AXES), P(AXES, None)),
        out_specs=(P(None, AXES), P(AXES)),
        check_vma=False,
    )
```

```python
import functools

import jax
import jax.numpy as jnp
from jax import lax
from jax.experimental import pallas as pl
from jax.experimental.pallas import tpu as pltpu
from jax.sharding import PartitionSpec as P

PTS = 64
NEIGH = 8
SPAN = 16
BLK = 2
WIDE = 128
SQRT_THREE = 1.7320508075688772
NUGGET = 0.25
AXES = ("group", "shard")
SLAB = 4
WINDOW = SPAN // SLAB + 1
COND = NEIGH * PTS
STEPS = COND // WIDE
HIGHEST = lax.Precision.HIGHEST
HIGH = lax.Precision.HIGH
F32 = jnp.float32


def dot(a, b, dims=((1,), (0,)), precision=HIGHEST):
    return lax.dot_general(a, b, (dims, ((), ())), precision=precision, preferred_element_type=F32)


def quick(a, b, dims=((1,), (0,))):
    return dot(a, b, dims, HIGH)


def iota(shape, dim):
    return lax.broadcasted_iota(jnp.int32, shape, dim)


def eye(n):
    return (iota((n, n), 0) == iota((n, n), 1)).astype(F32)


def schedule(low, high):
    rho = (high - low) / (high + low)
    factors = []
    while rho > 3e-4:
        factors.append(2.0 / (2.0 - rho * rho))
        rho = rho * rho / (2.0 - rho * rho)
    return 2.0 / (low + high), factors


def inverses(mats):
    n = mats[0].shape[0]
    alpha, factors = schedule(0.245, n + 0.26)
    ident = eye(n)
    rs = [ident - alpha * m for m in mats]
    c = factors[0]
    xs = [(alpha * c) * (ident + r) for r in rs]
    rs = [(1.0 - c) * ident + c * quick(r, r) for r in rs]
    for c in factors[1:-1]:
        nxt = [c * (x + quick(x, r)) for x, r in zip(xs, rs)]
        rs = [(1.0 - c) * ident + c * quick(r, r) for r in rs]
        xs = nxt
    c = factors[-1]
    xs = [c * (x + quick(x, r)) for x, r in zip(xs, rs)]
    es = [ident - dot(m, x) for m, x in zip(mats, xs)]
    return [x + quick(x, e) for x, e in zip(xs, es)]


def kernel_value(dx, dy):
    s = SQRT_THREE * jnp.sqrt(dx * dx + dy * dy)
    return (1.0 + s) * jnp.exp(-s)


def place_of(me, device):
    return (lax.div(me, SLAB) - lax.div(device, SLAB)) * SLAB + (lax.rem(device, SLAB) ^ lax.rem(me, SLAB))


def factor_kernel(where_ref, nb_ref, coords_ref, g_ref, s_ref):
    me = where_ref[0]
    lane = iota((1, WIDE), 1)
    low = lane < PTS

    def half_row(dev, half, coord, to_low):
        row = coords_ref[dev, pl.ds(coord, 1), :]
        swapped = pltpu.roll(row, PTS, 1)
        take = half if to_low else 1 - half
        return jnp.where(take == 1, swapped, row)

    def column(row):
        return jnp.transpose(jnp.broadcast_to(row, (WIDE, WIDE)))

    mats = []
    for b in range(BLK):
        rows, valid = [], []
        for k in range(STEPS):
            pieces, oks = [], []
            for h in range(2):
                ident = nb_ref[b, 2 * k + h]
                ok = ident >= 0
                safe = jnp.where(ok, ident, me * BLK)
                dev, half = lax.div(safe, BLK), lax.rem(safe, BLK)
                pieces.append([half_row(dev, half, c, h == 0) for c in range(2)])
                oks.append(jnp.where(ok, 1.0, 0.0).astype(F32))
            rows.append([jnp.where(low, pieces[0][c], pieces[1][c]) for c in range(2)])
            valid.append(jnp.where(low, oks[0], oks[1]))
        own = [half_row(me, b, c, True) for c in range(2)]
        cols = [[column(r) for r in row] for row in rows]
        own_cols = [column(r)[:PTS, :PTS] for r in own]
        valid_cols = [column(v) for v in valid]
        mat = {}
        for i in range(STEPS):
            for j in range(i, STEPS):
                value = kernel_value(cols[i][0] - rows[j][0], cols[i][1] - rows[j][1])
                value = valid_cols[i] * valid[j] * value
                if i == j:
                    value = value + eye(WIDE) * (NUGGET * valid[j] + (1.0 - valid[j]))
                mat[i, j] = value
            value = kernel_value(cols[i][0][:, :PTS] - own[0][:, :PTS], cols[i][1][:, :PTS] - own[1][:, :PTS])
            mat[i, STEPS] = valid_cols[i][:, :PTS] * value
        value = kernel_value(own_cols[0] - own[0][:, :PTS], own_cols[1] - own[1][:, :PTS])
        mat[STEPS, STEPS] = value + NUGGET * eye(PTS)
        mats.append(mat)
    panels = [{} for _ in range(BLK)]
    for k in range(STEPS):
        invs = inverses([m[k, k] for m in mats])
        for j in range(k + 1, STEPS + 1):
            for b in range(BLK):
                panels[b][k, j] = dot(invs[b], mats[b][k, j])
        for i in range(k + 1, STEPS + 1):
            for j in range(i, STEPS + 1):
                for b in range(BLK):
                    mats[b][i, j] = mats[b][i, j] - dot(mats[b][k, i], panels[b][k, j], ((0,), (0,)))
    solved = [{} for _ in range(BLK)]
    for k in reversed(range(STEPS)):
        for b in range(BLK):
            total = panels[b][k, STEPS]
            for j in range(k + 1, STEPS):
                total = total - dot(panels[b][k, j], solved[b][j])
            solved[b][k] = total
    schur = [m[STEPS, STEPS] for m in mats]
    schur_inv = inverses(schur)
    g_ref[COND:, :] = jnp.concatenate(schur_inv, axis=1)
    for k in range(STEPS):
        g_ref[k * WIDE : (k + 1) * WIDE, :] = -jnp.concatenate([s[k] for s in solved], axis=1)
    s_ref[...] = jnp.concatenate(schur, axis=1)


def apply_kernel(where_ref, ids_ref, *rest):
    windows, w_refs, outs = rest[:WINDOW], rest[WINDOW : WINDOW + SLAB], rest[WINDOW + SLAB : -2]
    held, total = rest[-2], rest[-1]
    me = where_ref[0]
    slab, quarter = lax.div(me, SLAB), lax.rem(me, SLAB)
    low = iota((PTS, WIDE), 1) < PTS
    for o in range(WINDOW):
        held[o * SLAB : (o + 1) * SLAB] = windows[o][...]
    total[...] = jnp.zeros_like(total)

    for k in range(SLAB):
        sender = quarter ^ k
        device = slab * SLAB + sender
        places = []
        for b in range(BLK):
            for m in range(NEIGH):
                ident = ids_ref[sender, b, m]
                ident = jnp.where(ident >= 0, ident, device * BLK)
                owner = lax.div(ident, BLK)
                place = place_of(me, owner)
                turn = (lax.rem(ident, BLK) ^ (m % 2)) * PTS
                places.append((place, turn))
        gathered = []
        for b in range(BLK):
            pieces = []
            for m in range(0, NEIGH, 2):
                (p0, t0), (p1, t1) = places[b * NEIGH + m], places[b * NEIGH + m + 1]
                first = pltpu.roll(held[p0], t0, 1)
                second = pltpu.roll(held[p1], t1, 1)
                pieces.append(jnp.where(low, first, second))
            gathered.append(jnp.concatenate(pieces, axis=1))
        w = w_refs[k][:COND, :]
        white = quick(jnp.concatenate(gathered, axis=0), w)
        white = held[k] + jnp.where(low, white[:PTS], white[PTS:])
        v = w_refs[k][COND:, :]
        inv = jnp.concatenate([jnp.where(low, v, 0.0), jnp.where(low, 0.0, v)], axis=0)
        scaled = dot(white, inv)
        total[k] += scaled
        sides = jnp.concatenate([jnp.where(low, scaled, 0.0), jnp.where(low, 0.0, scaled)], axis=0)
        back = quick(sides, w, ((1,), (1,)))
        for b in range(BLK):
            for m in range(NEIGH):
                place, turn = places[b * NEIGH + m]
                tile = back[b * PTS : (b + 1) * PTS, (m // 2) * WIDE : (m // 2 + 1) * WIDE]
                tile = jnp.where(low, tile, 0.0) if m % 2 == 0 else jnp.where(low, 0.0, tile)
                total[place] += pltpu.roll(tile, turn, 1)
    for o in range(WINDOW):
        outs[o][...] = total[o * SLAB : (o + 1) * SLAB]


def logdet_kernel(s_ref, out_ref, work):
    work[...] = s_ref[...]
    rows = iota((PTS, WIDE), 0)
    lanes = iota((PTS, WIDE), 1)

    def step(k, total):
        mat = work[...]
        row = work[pl.ds(k, 1), :]
        first = jnp.sum(jnp.where(lanes == k, mat, 0.0), axis=1, keepdims=True)
        second = jnp.sum(jnp.where(lanes == k + PTS, mat, 0.0), axis=1, keepdims=True)
        col = jnp.where(lanes < PTS, first, second)
        pivot = jnp.sum(jnp.where(rows == k, col, 0.0), axis=0, keepdims=True)
        work[...] = mat - col * (row / pivot)
        return total + jnp.log(pivot)

    total = lax.fori_loop(0, PTS, step, jnp.zeros((1, WIDE), F32))
    out_ref[...] = jnp.broadcast_to(total * (1.0 / PTS), out_ref.shape)


def prepare_kernel(where_ref, coords_ref, nb_ref, probes_ref, told_ref, *outs_and_scratch):
    outs, scratch = outs_and_scratch[:-1], outs_and_scratch[-1]
    quarter = lax.rem(where_ref[0], SLAB)
    rows = outs[0].shape[0]
    scratch[...] = jnp.zeros_like(scratch)
    scratch[:2, :] = coords_ref[...]
    scratch[2 : 2 + BLK, :NEIGH] = nb_ref[...].astype(F32)
    told_ref[...] = jnp.broadcast_to(scratch[...][None], told_ref.shape)
    for k in range(SLAB):
        outs[k][...] = probes_ref[pl.ds(pl.multiple_of((quarter ^ k) * rows, rows), rows), :]


def sum_kernel(*refs):
    terms, outs = refs[:WINDOW], refs[WINDOW:]
    for k in range(SLAB):
        value = terms[0][k]
        for o in range(1, WINDOW):
            value = value + terms[o][k]
        outs[k][...] = value


def place_kernel(where_ref, *refs):
    tiles, out_ref = refs[:SLAB], refs[SLAB]
    quarter = lax.rem(where_ref[0], SLAB)
    rows = tiles[0].shape[0]
    for k in range(SLAB):
        out_ref[pl.ds(pl.multiple_of((quarter ^ k) * rows, rows), rows), :] = tiles[k][...]


def passed(value, by):
    size = lax.axis_size(AXES)
    return lax.ppermute(value, AXES, [(i, i + by) for i in range(size) if 0 <= i + by < size])


def swapped(value, mask):
    size = lax.axis_size(AXES)
    return lax.ppermute(value, AXES, [(i, i ^ mask) for i in range(size)])


def local(kernel, name, outs, specs, scratch=(), gflops=1):
    vmem = pl.BlockSpec(memory_space=pltpu.VMEM)
    return pl.pallas_call(
        kernel,
        out_shape=outs,
        in_specs=specs,
        out_specs=jax.tree.map(lambda _: vmem, outs),
        scratch_shapes=list(scratch),
        compiler_params=pltpu.CompilerParams(vmem_limit_bytes=32 * 2**20),
        cost_estimate=pl.CostEstimate(flops=gflops * 10**9, bytes_accessed=10**5, transcendentals=0),
        name=name,
    )


def shards(coords, probes, neighbours):
    count = lax.axis_size(AXES)
    quarter = probes.shape[0] // SLAB
    device = lax.axis_index(AXES)
    here = jnp.reshape(device, (1,)).astype(jnp.int32)
    smem = pl.BlockSpec(memory_space=pltpu.SMEM)
    vmem = pl.BlockSpec(memory_space=pltpu.VMEM)
    tile = jax.ShapeDtypeStruct((quarter, WIDE), F32)
    tiles = jax.ShapeDtypeStruct((SLAB, quarter, WIDE), F32)
    square = jax.ShapeDtypeStruct((PTS, WIDE), F32)

    told, *pieces = local(
        prepare_kernel,
        "prepare",
        (jax.ShapeDtypeStruct((count, 8, WIDE), F32),) + (tile,) * SLAB,
        [smem, vmem, vmem, vmem],
        [pltpu.VMEM((8, WIDE), F32)],
    )(here, coords, neighbours, probes)
    own = jnp.stack([pieces[0]] + [swapped(pieces[k], k) for k in range(1, SLAB)])
    everywhere = lax.all_to_all(told, AXES, 0, 0)
    ids = lax.dynamic_slice(everywhere, (device // SLAB * SLAB, 2, 0), (SLAB, BLK, NEIGH)).astype(jnp.int32)
    early = [passed(own, SLAB * o) for o in (3, 2)]
    w, schur = local(
        factor_kernel,
        "factor",
        (jax.ShapeDtypeStruct((COND + PTS, WIDE), F32), square),
        [smem, smem, vmem],
        gflops=14,
    )(here, neighbours, everywhere)
    w, own, *early = lax.optimization_barrier((w, own, *early))
    w_y = swapped(w, 2)
    late = [passed(own, SLAB), passed(own, SPAN)]
    w_d = swapped(w, 1)
    w_y, *late = lax.optimization_barrier((w_y, *late))
    window = [own, late[0], early[1], early[0], late[1]]
    w_yd = swapped(w_y, 1)
    terms = local(
        apply_kernel,
        "apply",
        (tiles,) * WINDOW,
        [smem, smem] + [vmem] * (WINDOW + SLAB),
        [pltpu.VMEM((WINDOW * SLAB, quarter, WIDE), F32)] * 2,
        gflops=4,
    )(here, ids, *window, w, w_d, w_y, w_yd)
    logs = local(
        logdet_kernel, "logdet", jax.ShapeDtypeStruct((8, WIDE), F32), [vmem], [pltpu.VMEM((PTS, WIDE), F32)], gflops=9
    )(schur)
    returned = [passed(terms[o], -SLAB * o) for o in (3, 2, 4, 1)]
    kept, logs = lax.optimization_barrier((terms[0], logs))
    sums = local(sum_kernel, "sum", (tile,) * SLAB, [vmem] * WINDOW)(kept, *returned)
    result = local(place_kernel, "place", jax.ShapeDtypeStruct(probes.shape, F32), [smem] + [vmem] * SLAB)(
        here, sums[0], *(swapped(sums[k], k) for k in range(1, SLAB))
    )
    return result, logs[0, :: PTS]


def solution(mesh):
    return jax.shard_map(
        shards,
        mesh=mesh,
        in_specs=(P(None, AXES), P(None, AXES), P(AXES, None)),
        out_specs=(P(None, AXES), P(AXES)),
        check_vma=False,
    )
```

```python
import functools

import jax
import jax.numpy as jnp
from jax import lax
from jax.experimental import pallas as pl
from jax.experimental.pallas import tpu as pltpu
from jax.sharding import PartitionSpec as P

PTS = 64
NEIGH = 8
SPAN = 16
BLK = 2
WIDE = 128
SQRT_THREE = 1.7320508075688772
NUGGET = 0.25
AXES = ("group", "shard")
SLAB = 4
WINDOW = SPAN // SLAB + 1
COND = NEIGH * PTS
STEPS = COND // WIDE
HIGHEST = lax.Precision.HIGHEST
HIGH = lax.Precision.HIGH
F32 = jnp.float32


def dot(a, b, dims=((1,), (0,)), precision=HIGHEST):
    return lax.dot_general(a, b, (dims, ((), ())), precision=precision, preferred_element_type=F32)


def quick(a, b, dims=((1,), (0,))):
    return dot(a, b, dims, HIGH)


def iota(shape, dim):
    return lax.broadcasted_iota(jnp.int32, shape, dim)


def eye(n):
    return (iota((n, n), 0) == iota((n, n), 1)).astype(F32)


def schedule(low, high):
    rho = (high - low) / (high + low)
    factors = []
    while rho > 3e-4:
        factors.append(2.0 / (2.0 - rho * rho))
        rho = rho * rho / (2.0 - rho * rho)
    return 2.0 / (low + high), factors


def split(a):
    high = a.astype(jnp.bfloat16)
    return high, (a - high.astype(F32)).astype(jnp.bfloat16)


def products(lefts, right):
    high, low = split(right)
    rows = [jnp.concatenate([h, low_part, h], axis=1) for h, low_part in map(split, lefts)]
    out = lax.dot_general(
        jnp.concatenate(rows, axis=0),
        jnp.concatenate([high, high, low], axis=0),
        (((1,), (0,)), ((), ())),
        preferred_element_type=F32,
    )
    n = right.shape[0]
    return [out[i * n : (i + 1) * n] for i in range(len(lefts))]


def inverses(mats, top, tasks):
    alpha, factors = schedule(0.245, top + 0.26)
    stages = len(factors) + 1

    def spread(stage):
        for task in tasks[stage * len(tasks) // stages : (stage + 1) * len(tasks) // stages]:
            task()

    ident = eye(WIDE)
    rs = [ident - alpha * m for m in mats]
    c = factors[0]
    xs = [(alpha * c) * (ident + r) for r in rs]
    rs = [(1.0 - c) * ident + c * products([r], r)[0] for r in rs]
    spread(0)
    for stage, c in enumerate(factors[1:-1]):
        pairs = [products([x, r], r) for x, r in zip(xs, rs)]
        xs = [c * (x + xr) for x, (xr, _) in zip(xs, pairs)]
        rs = [(1.0 - c) * ident + c * rr for _, rr in pairs]
        spread(stage + 1)
    c = factors[-1]
    xs = [c * (x + products([x], r)[0]) for x, r in zip(xs, rs)]
    spread(stages - 2)
    es = [ident - dot(m, x) for m, x in zip(mats, xs)]
    spread(stages - 1)
    return [x + products([x], e)[0] for x, e in zip(xs, es)]


def kernel_value(dx, dy):
    s = SQRT_THREE * jnp.sqrt(dx * dx + dy * dy)
    return (1.0 + s) * jnp.exp(-s)


def place_of(me, device):
    return (lax.div(me, SLAB) - lax.div(device, SLAB)) * SLAB + (lax.rem(device, SLAB) ^ lax.rem(me, SLAB))


def factor_kernel(where_ref, nb_ref, coords_ref, g_ref, s_ref):
    me = where_ref[0]
    lane = iota((1, WIDE), 1)
    low = lane < PTS

    def half_row(dev, half, coord, to_low):
        row = coords_ref[dev, pl.ds(coord, 1), :]
        swapped = pltpu.roll(row, PTS, 1)
        take = half if to_low else 1 - half
        return jnp.where(take == 1, swapped, row)

    def column(row):
        return jnp.transpose(jnp.broadcast_to(row, (WIDE, WIDE)))

    points = []
    for b in range(BLK):
        rows, valid = [], []
        for k in range(STEPS):
            pieces, oks = [], []
            for h in range(2):
                ident = nb_ref[b, 2 * k + h]
                ok = ident >= 0
                safe = jnp.where(ok, ident, me * BLK)
                dev, half = lax.div(safe, BLK), lax.rem(safe, BLK)
                pieces.append([half_row(dev, half, c, h == 0) for c in range(2)])
                oks.append(jnp.where(ok, 1.0, 0.0).astype(F32))
            rows.append([jnp.where(low, pieces[0][c], pieces[1][c]) for c in range(2)])
            valid.append(jnp.where(low, oks[0], oks[1]))
        own = [half_row(me, b, c, True) for c in range(2)]
        cols = [[column(r) for r in row] for row in rows]
        own_cols = [column(r)[:PTS, :PTS] for r in own]
        valid_cols = [column(v) for v in valid]
        points.append((rows, valid, own, cols, own_cols, valid_cols))

    mats = [{} for _ in range(BLK)]
    panels = [{} for _ in range(BLK)]
    solved = [{} for _ in range(BLK)]

    def covariance(b, i, j):
        rows, valid, own, cols, own_cols, valid_cols = points[b]
        if i == STEPS:
            value = kernel_value(own_cols[0] - own[0][:, :PTS], own_cols[1] - own[1][:, :PTS])
            value = value + NUGGET * eye(PTS)
        elif j == STEPS:
            value = kernel_value(cols[i][0][:, :PTS] - own[0][:, :PTS], cols[i][1][:, :PTS] - own[1][:, :PTS])
            value = valid_cols[i][:, :PTS] * value
        else:
            value = kernel_value(cols[i][0] - rows[j][0], cols[i][1] - rows[j][1])
            value = valid_cols[i] * valid[j] * value
            if i == j:
                value = value + eye(WIDE) * (NUGGET * valid[j] + (1.0 - valid[j]))
        mats[b][i, j] = value

    def panel(b, k, j, inv):
        panels[b][k, j] = dot(inv, mats[b][k, j])

    def update(b, k, i, j):
        mats[b][i, j] = mats[b][i, j] - dot(mats[b][k, i], panels[b][k, j], ((0,), (0,)))

    def substitute(b, k):
        total = panels[b][k, STEPS]
        for j in range(k + 1, STEPS):
            total = total - dot(panels[b][k, j], solved[b][j])
        solved[b][k] = total

    def store(k):
        g_ref[k * WIDE : (k + 1) * WIDE, :] = -jnp.concatenate([s[k] for s in solved], axis=1)

    blocks = range(BLK)
    for i in range(STEPS + 1):
        for j in range(i, STEPS + 1):
            for b in blocks:
                covariance(b, i, j)
    tasks = []
    for k in range(STEPS):
        invs = inverses([m[k, k] for m in mats], WIDE, tasks)
        for b in blocks:
            panel(b, k, k + 1, invs[b])
        for b in blocks:
            update(b, k, k + 1, k + 1)
        tasks = [functools.partial(panel, b, k, j, invs[b]) for j in range(k + 2, STEPS + 1) for b in blocks]
        tasks += [
            functools.partial(update, b, k, i, j)
            for i in range(k + 1, STEPS + 1)
            for j in range(i, STEPS + 1)
            for b in blocks
            if (i, j) != (k + 1, k + 1)
        ]
    for k in reversed(range(STEPS)):
        tasks += [functools.partial(substitute, b, k) for b in blocks] + [functools.partial(store, k)]
    schur = [m[STEPS, STEPS] for m in mats]
    gap = jnp.zeros((PTS, PTS), F32)
    both = jnp.concatenate(
        [jnp.concatenate([schur[0], gap], axis=1), jnp.concatenate([gap, schur[1]], axis=1)], axis=0
    )
    both = inverses([both], PTS, tasks)[0]
    g_ref[COND:, :] = jnp.where(low, both[:PTS], both[PTS:])
    s_ref[...] = jnp.concatenate(schur, axis=1)


def apply_kernel(where_ref, ids_ref, *rest):
    windows, w_refs, outs = rest[:WINDOW], rest[WINDOW : WINDOW + SLAB], rest[WINDOW + SLAB : -2]
    held, total = rest[-2], rest[-1]
    me = where_ref[0]
    slab, quarter = lax.div(me, SLAB), lax.rem(me, SLAB)
    low = iota((PTS, WIDE), 1) < PTS
    for o in range(WINDOW):
        held[o * SLAB : (o + 1) * SLAB] = windows[o][...]
    total[...] = jnp.zeros_like(total)

    for k in range(SLAB):
        sender = quarter ^ k
        device = slab * SLAB + sender
        places = []
        for b in range(BLK):
            for m in range(NEIGH):
                ident = ids_ref[sender, b, m]
                ident = jnp.where(ident >= 0, ident, device * BLK)
                owner = lax.div(ident, BLK)
                place = place_of(me, owner)
                turn = (lax.rem(ident, BLK) ^ (m % 2)) * PTS
                places.append((place, turn))
        gathered = []
        for b in range(BLK):
            pieces = []
            for m in range(0, NEIGH, 2):
                (p0, t0), (p1, t1) = places[b * NEIGH + m], places[b * NEIGH + m + 1]
                first = pltpu.roll(held[p0], t0, 1)
                second = pltpu.roll(held[p1], t1, 1)
                pieces.append(jnp.where(low, first, second))
            gathered.append(jnp.concatenate(pieces, axis=1))
        w = w_refs[k][:COND, :]
        white = quick(jnp.concatenate(gathered, axis=0), w)
        white = held[k] + jnp.where(low, white[:PTS], white[PTS:])
        v = w_refs[k][COND:, :]
        inv = jnp.concatenate([jnp.where(low, v, 0.0), jnp.where(low, 0.0, v)], axis=0)
        scaled = dot(white, inv)
        total[k] += scaled
        sides = jnp.concatenate([jnp.where(low, scaled, 0.0), jnp.where(low, 0.0, scaled)], axis=0)
        back = quick(sides, w, ((1,), (1,)))
        for b in range(BLK):
            for m in range(NEIGH):
                place, turn = places[b * NEIGH + m]
                tile = back[b * PTS : (b + 1) * PTS, (m // 2) * WIDE : (m // 2 + 1) * WIDE]
                tile = jnp.where(low, tile, 0.0) if m % 2 == 0 else jnp.where(low, 0.0, tile)
                total[place] += pltpu.roll(tile, turn, 1)
    for o in range(WINDOW):
        outs[o][...] = total[o * SLAB : (o + 1) * SLAB]


def logdet_kernel(s_ref, out_ref, work):
    work[...] = s_ref[...]
    rows = iota((PTS, WIDE), 0)
    lanes = iota((PTS, WIDE), 1)

    def step(k, total):
        mat = work[...]
        row = work[pl.ds(k, 1), :]
        first = jnp.sum(jnp.where(lanes == k, mat, 0.0), axis=1, keepdims=True)
        second = jnp.sum(jnp.where(lanes == k + PTS, mat, 0.0), axis=1, keepdims=True)
        col = jnp.where(lanes < PTS, first, second)
        pivot = jnp.sum(jnp.where(rows == k, col, 0.0), axis=0, keepdims=True)
        work[...] = mat - col * (row / pivot)
        return total + jnp.log(pivot)

    total = lax.fori_loop(0, PTS, step, jnp.zeros((1, WIDE), F32))
    out_ref[...] = jnp.broadcast_to(total * (1.0 / PTS), out_ref.shape)


def prepare_kernel(where_ref, coords_ref, nb_ref, probes_ref, told_ref, *outs_and_scratch):
    outs, scratch = outs_and_scratch[:-1], outs_and_scratch[-1]
    quarter = lax.rem(where_ref[0], SLAB)
    rows = outs[0].shape[0]
    scratch[...] = jnp.zeros_like(scratch)
    scratch[:2, :] = coords_ref[...]
    scratch[2 : 2 + BLK, :NEIGH] = nb_ref[...].astype(F32)
    told_ref[...] = jnp.broadcast_to(scratch[...][None], told_ref.shape)
    for k in range(SLAB):
        outs[k][...] = probes_ref[pl.ds(pl.multiple_of((quarter ^ k) * rows, rows), rows), :]


def sum_kernel(*refs):
    terms, outs = refs[:WINDOW], refs[WINDOW:]
    for k in range(SLAB):
        value = terms[0][k]
        for o in range(1, WINDOW):
            value = value + terms[o][k]
        outs[k][...] = value


def place_kernel(where_ref, *refs):
    tiles, out_ref = refs[:SLAB], refs[SLAB]
    quarter = lax.rem(where_ref[0], SLAB)
    rows = tiles[0].shape[0]
    for k in range(SLAB):
        out_ref[pl.ds(pl.multiple_of((quarter ^ k) * rows, rows), rows), :] = tiles[k][...]


def passed(value, by):
    size = lax.axis_size(AXES)
    return lax.ppermute(value, AXES, [(i, i + by) for i in range(size) if 0 <= i + by < size])


def swapped(value, mask):
    size = lax.axis_size(AXES)
    return lax.ppermute(value, AXES, [(i, i ^ mask) for i in range(size)])


def local(kernel, name, outs, specs, scratch=(), gflops=1):
    vmem = pl.BlockSpec(memory_space=pltpu.VMEM)
    return pl.pallas_call(
        kernel,
        out_shape=outs,
        in_specs=specs,
        out_specs=jax.tree.map(lambda _: vmem, outs),
        scratch_shapes=list(scratch),
        compiler_params=pltpu.CompilerParams(vmem_limit_bytes=32 * 2**20),
        cost_estimate=pl.CostEstimate(flops=gflops * 10**9, bytes_accessed=10**5, transcendentals=0),
        name=name,
    )


def shards(coords, probes, neighbours):
    count = lax.axis_size(AXES)
    quarter = probes.shape[0] // SLAB
    device = lax.axis_index(AXES)
    here = jnp.reshape(device, (1,)).astype(jnp.int32)
    smem = pl.BlockSpec(memory_space=pltpu.SMEM)
    vmem = pl.BlockSpec(memory_space=pltpu.VMEM)
    tile = jax.ShapeDtypeStruct((quarter, WIDE), F32)
    tiles = jax.ShapeDtypeStruct((SLAB, quarter, WIDE), F32)
    square = jax.ShapeDtypeStruct((PTS, WIDE), F32)

    told, *pieces = local(
        prepare_kernel,
        "prepare",
        (jax.ShapeDtypeStruct((count, 8, WIDE), F32),) + (tile,) * SLAB,
        [smem, vmem, vmem, vmem],
        [pltpu.VMEM((8, WIDE), F32)],
    )(here, coords, neighbours, probes)
    own = jnp.stack([pieces[0]] + [swapped(pieces[k], k) for k in range(1, SLAB)])
    everywhere = lax.all_to_all(told, AXES, 0, 0)
    ids = lax.dynamic_slice(everywhere, (device // SLAB * SLAB, 2, 0), (SLAB, BLK, NEIGH)).astype(jnp.int32)
    early = [passed(own, SLAB * o) for o in (3, 2)]
    w, schur = local(
        factor_kernel,
        "factor",
        (jax.ShapeDtypeStruct((COND + PTS, WIDE), F32), square),
        [smem, smem, vmem],
        gflops=14,
    )(here, neighbours, everywhere)
    w, own, *early = lax.optimization_barrier((w, own, *early))
    w_y = swapped(w, 2)
    late = [passed(own, SLAB), passed(own, SPAN)]
    w_d = swapped(w, 1)
    w_y, *late = lax.optimization_barrier((w_y, *late))
    window = [own, late[0], early[1], early[0], late[1]]
    w_yd = swapped(w_y, 1)
    terms = local(
        apply_kernel,
        "apply",
        (tiles,) * WINDOW,
        [smem, smem] + [vmem] * (WINDOW + SLAB),
        [pltpu.VMEM((WINDOW * SLAB, quarter, WIDE), F32)] * 2,
        gflops=4,
    )(here, ids, *window, w, w_d, w_y, w_yd)
    logs = local(
        logdet_kernel, "logdet", jax.ShapeDtypeStruct((8, WIDE), F32), [vmem], [pltpu.VMEM((PTS, WIDE), F32)], gflops=9
    )(schur)
    returned = [passed(terms[o], -SLAB * o) for o in (3, 2, 4, 1)]
    kept, logs = lax.optimization_barrier((terms[0], logs))
    sums = local(sum_kernel, "sum", (tile,) * SLAB, [vmem] * WINDOW)(kept, *returned)
    result = local(place_kernel, "place", jax.ShapeDtypeStruct(probes.shape, F32), [smem] + [vmem] * SLAB)(
        here, sums[0], *(swapped(sums[k], k) for k in range(1, SLAB))
    )
    return result, logs[0, :: PTS]


def solution(mesh):
    return jax.shard_map(
        shards,
        mesh=mesh,
        in_specs=(P(None, AXES), P(None, AXES), P(AXES, None)),
        out_specs=(P(None, AXES), P(AXES)),
        check_vma=False,
    )
```

```python
import functools

import jax
import jax.numpy as jnp
from jax import lax
from jax.experimental import pallas as pl
from jax.experimental.pallas import tpu as pltpu
from jax.sharding import PartitionSpec as P

PTS = 64
NEIGH = 8
SPAN = 16
BLK = 2
WIDE = 128
SQRT_THREE = 1.7320508075688772
NUGGET = 0.25
AXES = ("group", "shard")
SLAB = 4
WINDOW = SPAN // SLAB + 1
COND = NEIGH * PTS
STEPS = COND // WIDE
HIGHEST = lax.Precision.HIGHEST
HIGH = lax.Precision.HIGH
F32 = jnp.float32


def dot(a, b, dims=((1,), (0,)), precision=HIGHEST):
    return lax.dot_general(a, b, (dims, ((), ())), precision=precision, preferred_element_type=F32)


def quick(a, b, dims=((1,), (0,))):
    return dot(a, b, dims, HIGH)


def iota(shape, dim):
    return lax.broadcasted_iota(jnp.int32, shape, dim)


def eye(n):
    return (iota((n, n), 0) == iota((n, n), 1)).astype(F32)


def schedule(low, high):
    rho = (high - low) / (high + low)
    factors = []
    while rho > 3e-4:
        factors.append(2.0 / (2.0 - rho * rho))
        rho = rho * rho / (2.0 - rho * rho)
    return 2.0 / (low + high), factors


def split(a):
    high = a.astype(jnp.bfloat16)
    return high, (a - high.astype(F32)).astype(jnp.bfloat16)


def products(lefts, right):
    high, low = split(right)
    rows = [jnp.concatenate([h, low_part, h], axis=1) for h, low_part in map(split, lefts)]
    out = lax.dot_general(
        jnp.concatenate(rows, axis=0),
        jnp.concatenate([high, high, low], axis=0),
        (((1,), (0,)), ((), ())),
        preferred_element_type=F32,
    )
    n = right.shape[0]
    return [out[i * n : (i + 1) * n] for i in range(len(lefts))]


def inverses(mats, top, tasks):
    alpha, factors = schedule(0.245, top + 0.26)
    stages = len(factors) + 1

    def spread(stage):
        for task in tasks[stage * len(tasks) // stages : (stage + 1) * len(tasks) // stages]:
            task()

    ident = eye(WIDE)
    rs = [ident - alpha * m for m in mats]
    c = factors[0]
    xs = [(alpha * c) * (ident + r) for r in rs]
    rs = [(1.0 - c) * ident + c * products([r], r)[0] for r in rs]
    spread(0)
    for stage, c in enumerate(factors[1:-1]):
        pairs = [products([x, r], r) for x, r in zip(xs, rs)]
        xs = [c * (x + xr) for x, (xr, _) in zip(xs, pairs)]
        rs = [(1.0 - c) * ident + c * rr for _, rr in pairs]
        spread(stage + 1)
    c = factors[-1]
    xs = [c * (x + products([x], r)[0]) for x, r in zip(xs, rs)]
    spread(stages - 2)
    es = [ident - dot(m, x) for m, x in zip(mats, xs)]
    spread(stages - 1)
    return [x + products([x], e)[0] for x, e in zip(xs, es)]


def kernel_value(dx, dy):
    s = SQRT_THREE * jnp.sqrt(dx * dx + dy * dy)
    return (1.0 + s) * jnp.exp(-s)


def place_of(me, device):
    return (lax.div(me, SLAB) - lax.div(device, SLAB)) * SLAB + (lax.rem(device, SLAB) ^ lax.rem(me, SLAB))


def factor_kernel(where_ref, nb_ref, coords_ref, g_ref, s_ref):
    me = where_ref[0]
    lane = iota((1, WIDE), 1)
    low = lane < PTS

    def half_row(dev, half, coord, to_low):
        row = coords_ref[dev, pl.ds(coord, 1), :]
        swapped = pltpu.roll(row, PTS, 1)
        take = half if to_low else 1 - half
        return jnp.where(take == 1, swapped, row)

    def column(row):
        return jnp.transpose(jnp.broadcast_to(row, (WIDE, WIDE)))

    points = []
    for b in range(BLK):
        rows, valid = [], []
        for k in range(STEPS):
            pieces, oks = [], []
            for h in range(2):
                ident = nb_ref[b, 2 * k + h]
                ok = ident >= 0
                safe = jnp.where(ok, ident, me * BLK)
                dev, half = lax.div(safe, BLK), lax.rem(safe, BLK)
                pieces.append([half_row(dev, half, c, h == 0) for c in range(2)])
                oks.append(jnp.where(ok, 1.0, 0.0).astype(F32))
            rows.append([jnp.where(low, pieces[0][c], pieces[1][c]) for c in range(2)])
            valid.append(jnp.where(low, oks[0], oks[1]))
        own = [half_row(me, b, c, True) for c in range(2)]
        cols = [[column(r) for r in row] for row in rows]
        own_cols = [column(r)[:PTS, :PTS] for r in own]
        valid_cols = [column(v) for v in valid]
        points.append((rows, valid, own, cols, own_cols, valid_cols))

    mats = [{} for _ in range(BLK)]
    panels = [{} for _ in range(BLK)]
    solved = [{} for _ in range(BLK)]

    def covariance(b, i, j):
        rows, valid, own, cols, own_cols, valid_cols = points[b]
        if i == STEPS:
            value = kernel_value(own_cols[0] - own[0][:, :PTS], own_cols[1] - own[1][:, :PTS])
            value = value + NUGGET * eye(PTS)
        elif j == STEPS:
            value = kernel_value(cols[i][0][:, :PTS] - own[0][:, :PTS], cols[i][1][:, :PTS] - own[1][:, :PTS])
            value = valid_cols[i][:, :PTS] * value
        else:
            value = kernel_value(cols[i][0] - rows[j][0], cols[i][1] - rows[j][1])
            value = valid_cols[i] * valid[j] * value
            if i == j:
                value = value + eye(WIDE) * (NUGGET * valid[j] + (1.0 - valid[j]))
        mats[b][i, j] = value

    def panel(b, k, j, inv):
        panels[b][k, j] = dot(inv, mats[b][k, j])

    def update(b, k, i, j):
        mats[b][i, j] = mats[b][i, j] - dot(mats[b][k, i], panels[b][k, j], ((0,), (0,)))

    def substitute(b, k):
        total = panels[b][k, STEPS]
        for j in range(k + 1, STEPS):
            total = total - dot(panels[b][k, j], solved[b][j])
        solved[b][k] = total

    def store(k):
        g_ref[k * WIDE : (k + 1) * WIDE, :] = -jnp.concatenate([s[k] for s in solved], axis=1)

    blocks = range(BLK)
    for i in range(STEPS + 1):
        for j in range(i, STEPS + 1):
            for b in blocks:
                covariance(b, i, j)
    tasks = []
    for k in range(STEPS):
        invs = inverses([m[k, k] for m in mats], WIDE, tasks)
        for b in blocks:
            panel(b, k, k + 1, invs[b])
        for b in blocks:
            update(b, k, k + 1, k + 1)
        tasks = [functools.partial(panel, b, k, j, invs[b]) for j in range(k + 2, STEPS + 1) for b in blocks]
        tasks += [
            functools.partial(update, b, k, i, j)
            for i in range(k + 1, STEPS + 1)
            for j in range(i, STEPS + 1)
            for b in blocks
            if (i, j) != (k + 1, k + 1)
        ]
    for k in reversed(range(STEPS)):
        tasks += [functools.partial(substitute, b, k) for b in blocks] + [functools.partial(store, k)]
    schur = [m[STEPS, STEPS] for m in mats]
    gap = jnp.zeros((PTS, PTS), F32)
    both = jnp.concatenate(
        [jnp.concatenate([schur[0], gap], axis=1), jnp.concatenate([gap, schur[1]], axis=1)], axis=0
    )
    both = inverses([both], PTS, tasks)[0]
    g_ref[COND:, :] = jnp.where(low, both[:PTS], both[PTS:])
    s_ref[...] = jnp.concatenate(schur, axis=1)


def apply_kernel(where_ref, ids_ref, *rest):
    windows, w_refs, outs = rest[:WINDOW], rest[WINDOW : WINDOW + SLAB], rest[WINDOW + SLAB : -2]
    held, total = rest[-2], rest[-1]
    me = where_ref[0]
    slab, quarter = lax.div(me, SLAB), lax.rem(me, SLAB)
    low = iota((PTS, WIDE), 1) < PTS
    places_held = WINDOW * SLAB
    for o in range(WINDOW):
        for q in range(SLAB):
            tile = windows[o][q]
            held[o * SLAB + q] = tile
            held[places_held + o * SLAB + q] = pltpu.roll(tile, PTS, 1)
    total[...] = jnp.zeros_like(total)

    places = []
    for k in range(SLAB):
        device = slab * SLAB + (quarter ^ k)
        for b in range(BLK):
            for m in range(NEIGH):
                ident = ids_ref[quarter ^ k, b, m]
                ident = jnp.where(ident >= 0, ident, device * BLK)
                turned = lax.rem(ident, BLK) ^ (m % 2)
                places.append(place_of(me, lax.div(ident, BLK)) + turned * places_held)
    gathered = []
    for k in range(SLAB):
        sides = []
        for b in range(BLK):
            at = places[(k * BLK + b) * NEIGH : (k * BLK + b + 1) * NEIGH]
            pieces = [jnp.where(low, held[at[m]], held[at[m + 1]]) for m in range(0, NEIGH, 2)]
            sides.append(jnp.concatenate(pieces, axis=1))
        gathered.append(jnp.concatenate(sides, axis=0))
    whites = [quick(gathered[k], w_refs[k][:COND, :]) for k in range(SLAB)]
    scaled = []
    for k in range(SLAB):
        white = held[k] + jnp.where(low, whites[k][:PTS], whites[k][PTS:])
        v = w_refs[k][COND:, :]
        inv = jnp.concatenate([jnp.where(low, v, 0.0), jnp.where(low, 0.0, v)], axis=0)
        scaled.append(dot(white, inv))
    backs = []
    for k in range(SLAB):
        sides = jnp.concatenate([jnp.where(low, scaled[k], 0.0), jnp.where(low, 0.0, scaled[k])], axis=0)
        backs.append(quick(sides, w_refs[k][:COND, :], ((1,), (1,))))
    for k in range(SLAB):
        total[k] = scaled[k]
    for k in range(SLAB):
        for b in range(BLK):
            for m in range(NEIGH):
                tile = backs[k][b * PTS : (b + 1) * PTS, (m // 2) * WIDE : (m // 2 + 1) * WIDE]
                tile = jnp.where(low, tile, 0.0) if m % 2 == 0 else jnp.where(low, 0.0, tile)
                total[places[(k * BLK + b) * NEIGH + m]] += tile
    for o in range(WINDOW):
        for q in range(SLAB):
            place = o * SLAB + q
            outs[o][q] = total[place] + pltpu.roll(total[places_held + place], PTS, 1)


def logdet_kernel(s_ref, out_ref, work):
    work[...] = s_ref[...]
    rows = iota((PTS, WIDE), 0)
    lanes = iota((PTS, WIDE), 1)

    def step(k, total):
        mat = work[...]
        row = work[pl.ds(k, 1), :]
        first = jnp.sum(jnp.where(lanes == k, mat, 0.0), axis=1, keepdims=True)
        second = jnp.sum(jnp.where(lanes == k + PTS, mat, 0.0), axis=1, keepdims=True)
        col = jnp.where(lanes < PTS, first, second)
        pivot = jnp.sum(jnp.where(rows == k, col, 0.0), axis=0, keepdims=True)
        work[...] = mat - col * (row / pivot)
        return total + jnp.log(pivot)

    total = lax.fori_loop(0, PTS, step, jnp.zeros((1, WIDE), F32))
    out_ref[...] = jnp.broadcast_to(total * (1.0 / PTS), out_ref.shape)


def prepare_kernel(where_ref, coords_ref, nb_ref, probes_ref, told_ref, *outs_and_scratch):
    outs, scratch = outs_and_scratch[:-1], outs_and_scratch[-1]
    quarter = lax.rem(where_ref[0], SLAB)
    rows = outs[0].shape[0]
    scratch[...] = jnp.zeros_like(scratch)
    scratch[:2, :] = coords_ref[...]
    scratch[2 : 2 + BLK, :NEIGH] = nb_ref[...].astype(F32)
    told_ref[...] = jnp.broadcast_to(scratch[...][None], told_ref.shape)
    for k in range(SLAB):
        outs[k][...] = probes_ref[pl.ds(pl.multiple_of((quarter ^ k) * rows, rows), rows), :]


def sum_kernel(*refs):
    terms, outs = refs[:WINDOW], refs[WINDOW:]
    for k in range(SLAB):
        value = terms[0][k]
        for o in range(1, WINDOW):
            value = value + terms[o][k]
        outs[k][...] = value


def place_kernel(where_ref, *refs):
    tiles, out_ref = refs[:SLAB], refs[SLAB]
    quarter = lax.rem(where_ref[0], SLAB)
    rows = tiles[0].shape[0]
    for k in range(SLAB):
        out_ref[pl.ds(pl.multiple_of((quarter ^ k) * rows, rows), rows), :] = tiles[k][...]


def passed(value, by):
    size = lax.axis_size(AXES)
    return lax.ppermute(value, AXES, [(i, i + by) for i in range(size) if 0 <= i + by < size])


def swapped(value, mask):
    size = lax.axis_size(AXES)
    return lax.ppermute(value, AXES, [(i, i ^ mask) for i in range(size)])


def local(kernel, name, outs, specs, scratch=(), gflops=1):
    vmem = pl.BlockSpec(memory_space=pltpu.VMEM)
    return pl.pallas_call(
        kernel,
        out_shape=outs,
        in_specs=specs,
        out_specs=jax.tree.map(lambda _: vmem, outs),
        scratch_shapes=list(scratch),
        compiler_params=pltpu.CompilerParams(vmem_limit_bytes=32 * 2**20),
        cost_estimate=pl.CostEstimate(flops=gflops * 10**9, bytes_accessed=10**5, transcendentals=0),
        name=name,
    )


def shards(coords, probes, neighbours):
    count = lax.axis_size(AXES)
    quarter = probes.shape[0] // SLAB
    device = lax.axis_index(AXES)
    here = jnp.reshape(device, (1,)).astype(jnp.int32)
    smem = pl.BlockSpec(memory_space=pltpu.SMEM)
    vmem = pl.BlockSpec(memory_space=pltpu.VMEM)
    tile = jax.ShapeDtypeStruct((quarter, WIDE), F32)
    tiles = jax.ShapeDtypeStruct((SLAB, quarter, WIDE), F32)
    square = jax.ShapeDtypeStruct((PTS, WIDE), F32)

    told, *pieces = local(
        prepare_kernel,
        "prepare",
        (jax.ShapeDtypeStruct((count, 8, WIDE), F32),) + (tile,) * SLAB,
        [smem, vmem, vmem, vmem],
        [pltpu.VMEM((8, WIDE), F32)],
    )(here, coords, neighbours, probes)
    own = jnp.stack([pieces[0]] + [swapped(pieces[k], k) for k in range(1, SLAB)])
    everywhere = lax.all_to_all(told, AXES, 0, 0)
    ids = lax.dynamic_slice(everywhere, (device // SLAB * SLAB, 2, 0), (SLAB, BLK, NEIGH)).astype(jnp.int32)
    early = [passed(own, SLAB * o) for o in (3, 2)]
    w, schur = local(
        factor_kernel,
        "factor",
        (jax.ShapeDtypeStruct((COND + PTS, WIDE), F32), square),
        [smem, smem, vmem],
        gflops=14,
    )(here, neighbours, everywhere)
    w, own, *early = lax.optimization_barrier((w, own, *early))
    w_y = swapped(w, 2)
    late = [passed(own, SLAB), passed(own, SPAN)]
    w_d = swapped(w, 1)
    w_y, *late = lax.optimization_barrier((w_y, *late))
    window = [own, late[0], early[1], early[0], late[1]]
    w_yd = swapped(w_y, 1)
    terms = local(
        apply_kernel,
        "apply",
        (tiles,) * WINDOW,
        [smem, smem] + [vmem] * (WINDOW + SLAB),
        [pltpu.VMEM((2 * WINDOW * SLAB, quarter, WIDE), F32)] * 2,
        gflops=4,
    )(here, ids, *window, w, w_d, w_y, w_yd)
    logs = local(
        logdet_kernel, "logdet", jax.ShapeDtypeStruct((8, WIDE), F32), [vmem], [pltpu.VMEM((PTS, WIDE), F32)], gflops=9
    )(schur)
    returned = [passed(terms[o], -SLAB * o) for o in (3, 2, 4, 1)]
    kept, logs = lax.optimization_barrier((terms[0], logs))
    sums = local(sum_kernel, "sum", (tile,) * SLAB, [vmem] * WINDOW)(kept, *returned)
    result = local(place_kernel, "place", jax.ShapeDtypeStruct(probes.shape, F32), [smem] + [vmem] * SLAB)(
        here, sums[0], *(swapped(sums[k], k) for k in range(1, SLAB))
    )
    return result, logs[0, :: PTS]


def solution(mesh):
    return jax.shard_map(
        shards,
        mesh=mesh,
        in_specs=(P(None, AXES), P(None, AXES), P(AXES, None)),
        out_specs=(P(None, AXES), P(AXES)),
        check_vma=False,
    )
```

```python
import functools

import jax
import jax.numpy as jnp
from jax import lax
from jax.experimental import pallas as pl
from jax.experimental.pallas import tpu as pltpu
from jax.sharding import PartitionSpec as P

PTS = 64
NEIGH = 8
SPAN = 16
BLK = 2
WIDE = 128
SQRT_THREE = 1.7320508075688772
NUGGET = 0.25
AXES = ("group", "shard")
SLAB = 4
WINDOW = SPAN // SLAB + 1
COND = NEIGH * PTS
STEPS = COND // WIDE
HIGHEST = lax.Precision.HIGHEST
HIGH = lax.Precision.HIGH
F32 = jnp.float32


def dot(a, b, dims=((1,), (0,)), precision=HIGHEST):
    return lax.dot_general(a, b, (dims, ((), ())), precision=precision, preferred_element_type=F32)


def quick(a, b, dims=((1,), (0,))):
    return dot(a, b, dims, HIGH)


def iota(shape, dim):
    return lax.broadcasted_iota(jnp.int32, shape, dim)


def eye(n):
    return (iota((n, n), 0) == iota((n, n), 1)).astype(F32)


def schedule(low, high):
    rho = (high - low) / (high + low)
    factors = []
    while rho > 3e-4:
        factors.append(2.0 / (2.0 - rho * rho))
        rho = rho * rho / (2.0 - rho * rho)
    return 2.0 / (low + high), factors


def split(a):
    high = a.astype(jnp.bfloat16)
    return high, (a - high.astype(F32)).astype(jnp.bfloat16)


def products(lefts, right):
    high, low = split(right)
    rows = [jnp.concatenate([h, low_part, h], axis=1) for h, low_part in map(split, lefts)]
    out = lax.dot_general(
        jnp.concatenate(rows, axis=0),
        jnp.concatenate([high, high, low], axis=0),
        (((1,), (0,)), ((), ())),
        preferred_element_type=F32,
    )
    n = right.shape[0]
    return [out[i * n : (i + 1) * n] for i in range(len(lefts))]


def inverses(mats, top, tasks):
    alpha, factors = schedule(0.245, top + 0.26)
    stages = len(factors) + 1

    def spread(stage):
        for task in tasks[stage * len(tasks) // stages : (stage + 1) * len(tasks) // stages]:
            task()

    ident = eye(WIDE)
    rs = [ident - alpha * m for m in mats]
    c = factors[0]
    xs = [(alpha * c) * (ident + r) for r in rs]
    rs = [(1.0 - c) * ident + c * products([r], r)[0] for r in rs]
    spread(0)
    for stage, c in enumerate(factors[1:-1]):
        pairs = [products([x, r], r) for x, r in zip(xs, rs)]
        xs = [c * (x + xr) for x, (xr, _) in zip(xs, pairs)]
        rs = [(1.0 - c) * ident + c * rr for _, rr in pairs]
        spread(stage + 1)
    c = factors[-1]
    xs = [c * (x + products([x], r)[0]) for x, r in zip(xs, rs)]
    spread(stages - 2)
    es = [ident - dot(m, x) for m, x in zip(mats, xs)]
    spread(stages - 1)
    return [x + products([x], e)[0] for x, e in zip(xs, es)]


def kernel_value(dx, dy):
    s = SQRT_THREE * jnp.sqrt(dx * dx + dy * dy)
    return (1.0 + s) * jnp.exp(-s)


def place_of(me, device):
    return (lax.div(me, SLAB) - lax.div(device, SLAB)) * SLAB + (lax.rem(device, SLAB) ^ lax.rem(me, SLAB))


def factor_kernel(where_ref, nb_ref, coords_ref, g_ref, s_ref):
    me = where_ref[0]
    lane = iota((1, WIDE), 1)
    low = lane < PTS

    def half_row(dev, half, coord, to_low):
        row = coords_ref[dev, pl.ds(coord, 1), :]
        swapped = pltpu.roll(row, PTS, 1)
        take = half if to_low else 1 - half
        return jnp.where(take == 1, swapped, row)

    def column(row):
        return jnp.transpose(jnp.broadcast_to(row, (WIDE, WIDE)))

    points = []
    for b in range(BLK):
        rows, valid = [], []
        for k in range(STEPS):
            pieces, oks = [], []
            for h in range(2):
                ident = nb_ref[b, 2 * k + h]
                ok = ident >= 0
                safe = jnp.where(ok, ident, me * BLK)
                dev, half = lax.div(safe, BLK), lax.rem(safe, BLK)
                pieces.append([half_row(dev, half, c, h == 0) for c in range(2)])
                oks.append(jnp.where(ok, 1.0, 0.0).astype(F32))
            rows.append([jnp.where(low, pieces[0][c], pieces[1][c]) for c in range(2)])
            valid.append(jnp.where(low, oks[0], oks[1]))
        own = [half_row(me, b, c, True) for c in range(2)]
        cols = [[column(r) for r in row] for row in rows]
        own_cols = [column(r)[:PTS, :PTS] for r in own]
        valid_cols = [column(v) for v in valid]
        points.append((rows, valid, own, cols, own_cols, valid_cols))

    mats = [{} for _ in range(BLK)]
    panels = [{} for _ in range(BLK)]
    solved = [{} for _ in range(BLK)]

    def covariance(b, i, j):
        rows, valid, own, cols, own_cols, valid_cols = points[b]
        if i == STEPS:
            value = kernel_value(own_cols[0] - own[0][:, :PTS], own_cols[1] - own[1][:, :PTS])
            value = value + NUGGET * eye(PTS)
        elif j == STEPS:
            value = kernel_value(cols[i][0][:, :PTS] - own[0][:, :PTS], cols[i][1][:, :PTS] - own[1][:, :PTS])
            value = valid_cols[i][:, :PTS] * value
        else:
            value = kernel_value(cols[i][0] - rows[j][0], cols[i][1] - rows[j][1])
            value = valid_cols[i] * valid[j] * value
            if i == j:
                value = value + eye(WIDE) * (NUGGET * valid[j] + (1.0 - valid[j]))
        mats[b][i, j] = value

    def panel(b, k, j, inv):
        panels[b][k, j] = dot(inv, mats[b][k, j])

    def update(b, k, i, j):
        mats[b][i, j] = mats[b][i, j] - dot(mats[b][k, i], panels[b][k, j], ((0,), (0,)))

    def substitute(b, k):
        total = panels[b][k, STEPS]
        for j in range(k + 1, STEPS):
            total = total - dot(panels[b][k, j], solved[b][j])
        solved[b][k] = total

    def store(k):
        g_ref[k * WIDE : (k + 1) * WIDE, :] = -jnp.concatenate([s[k] for s in solved], axis=1)

    blocks = range(BLK)
    for i in range(STEPS + 1):
        for j in range(i, STEPS + 1):
            for b in blocks:
                covariance(b, i, j)
    tasks = []
    for k in range(STEPS):
        invs = inverses([m[k, k] for m in mats], WIDE, tasks)
        for b in blocks:
            panel(b, k, k + 1, invs[b])
        for b in blocks:
            update(b, k, k + 1, k + 1)
        tasks = [functools.partial(panel, b, k, j, invs[b]) for j in range(k + 2, STEPS + 1) for b in blocks]
        tasks += [
            functools.partial(update, b, k, i, j)
            for i in range(k + 1, STEPS + 1)
            for j in range(i, STEPS + 1)
            for b in blocks
            if (i, j) != (k + 1, k + 1)
        ]
    for k in reversed(range(STEPS)):
        tasks += [functools.partial(substitute, b, k) for b in blocks] + [functools.partial(store, k)]
    schur = [m[STEPS, STEPS] for m in mats]
    gap = jnp.zeros((PTS, PTS), F32)
    both = jnp.concatenate(
        [jnp.concatenate([schur[0], gap], axis=1), jnp.concatenate([gap, schur[1]], axis=1)], axis=0
    )
    both = inverses([both], PTS, tasks)[0]
    g_ref[COND:, :] = jnp.where(low, both[:PTS], both[PTS:])
    s_ref[...] = jnp.concatenate(schur, axis=1)


def apply_kernel(where_ref, ids_ref, *rest):
    windows, w_refs, outs = rest[:WINDOW], rest[WINDOW : WINDOW + SLAB], rest[WINDOW + SLAB : -2]
    held, total = rest[-2], rest[-1]
    me = where_ref[0]
    slab, quarter = lax.div(me, SLAB), lax.rem(me, SLAB)
    low = iota((PTS, WIDE), 1) < PTS
    places_held = WINDOW * SLAB
    for o in range(WINDOW):
        for q in range(SLAB):
            tile = windows[o][q]
            held[o * SLAB + q] = tile
            held[places_held + o * SLAB + q] = pltpu.roll(tile, PTS, 1)
    total[...] = jnp.zeros_like(total)

    places = []
    for k in range(SLAB):
        device = slab * SLAB + (quarter ^ k)
        for b in range(BLK):
            for m in range(NEIGH):
                ident = ids_ref[quarter ^ k, b, m]
                ident = jnp.where(ident >= 0, ident, device * BLK)
                turned = lax.rem(ident, BLK) ^ (m % 2)
                places.append(place_of(me, lax.div(ident, BLK)) + turned * places_held)
    gathered = []
    for k in range(SLAB):
        sides = []
        for b in range(BLK):
            at = places[(k * BLK + b) * NEIGH : (k * BLK + b + 1) * NEIGH]
            pieces = [jnp.where(low, held[at[m]], held[at[m + 1]]) for m in range(0, NEIGH, 2)]
            sides.append(jnp.concatenate(pieces, axis=1))
        gathered.append(jnp.concatenate(sides, axis=0))
    whites = [quick(gathered[k], w_refs[k][:COND, :]) for k in range(SLAB)]
    scaled = []
    for k in range(SLAB):
        white = held[k] + jnp.where(low, whites[k][:PTS], whites[k][PTS:])
        v = w_refs[k][COND:, :]
        inv = jnp.concatenate([jnp.where(low, v, 0.0), jnp.where(low, 0.0, v)], axis=0)
        scaled.append(dot(white, inv))
    backs = []
    for k in range(SLAB):
        sides = jnp.concatenate([jnp.where(low, scaled[k], 0.0), jnp.where(low, 0.0, scaled[k])], axis=0)
        backs.append(quick(sides, w_refs[k][:COND, :], ((1,), (1,))))
    for k in range(SLAB):
        total[k] = scaled[k]
    for k in range(SLAB):
        for b in range(BLK):
            for m in range(NEIGH):
                tile = backs[k][b * PTS : (b + 1) * PTS, (m // 2) * WIDE : (m // 2 + 1) * WIDE]
                tile = jnp.where(low, tile, 0.0) if m % 2 == 0 else jnp.where(low, 0.0, tile)
                total[places[(k * BLK + b) * NEIGH + m]] += tile
    for o in range(WINDOW):
        for q in range(SLAB):
            place = o * SLAB + q
            outs[o][q] = total[place] + pltpu.roll(total[places_held + place], PTS, 1)


def logdet_kernel(s_ref, out_ref, work):
    work[...] = s_ref[...]
    rows = iota((PTS, WIDE), 0)
    lanes = iota((PTS, WIDE), 1)

    def step(k, total):
        mat = work[...]
        row = work[pl.ds(k, 1), :]
        first = jnp.sum(jnp.where(lanes == k, mat, 0.0), axis=1, keepdims=True)
        second = jnp.sum(jnp.where(lanes == k + PTS, mat, 0.0), axis=1, keepdims=True)
        col = jnp.where(lanes < PTS, first, second)
        pivot = jnp.sum(jnp.where(rows == k, col, 0.0), axis=0, keepdims=True)
        work[...] = mat - col * (row / pivot)
        return total + jnp.log(pivot)

    total = lax.fori_loop(0, PTS, step, jnp.zeros((1, WIDE), F32))
    out_ref[...] = jnp.broadcast_to(total * (1.0 / PTS), out_ref.shape)


def prepare_kernel(where_ref, probes_ref, *outs):
    quarter = lax.rem(where_ref[0], SLAB)
    rows = outs[0].shape[0]
    for k in range(SLAB):
        outs[k][...] = probes_ref[pl.ds(pl.multiple_of((quarter ^ k) * rows, rows), rows), :]


def sum_kernel(*refs):
    terms, outs = refs[:WINDOW], refs[WINDOW:]
    for k in range(SLAB):
        value = terms[0][k]
        for o in range(1, WINDOW):
            value = value + terms[o][k]
        outs[k][...] = value


def place_kernel(where_ref, *refs):
    tiles, out_ref = refs[:SLAB], refs[SLAB]
    quarter = lax.rem(where_ref[0], SLAB)
    rows = tiles[0].shape[0]
    for k in range(SLAB):
        out_ref[pl.ds(pl.multiple_of((quarter ^ k) * rows, rows), rows), :] = tiles[k][...]


def passed(value, by):
    size = lax.axis_size(AXES)
    return lax.ppermute(value, AXES, [(i, i + by) for i in range(size) if 0 <= i + by < size])


def swapped(value, mask):
    size = lax.axis_size(AXES)
    return lax.ppermute(value, AXES, [(i, i ^ mask) for i in range(size)])


def local(kernel, name, outs, specs, scratch=(), gflops=1):
    vmem = pl.BlockSpec(memory_space=pltpu.VMEM)
    return pl.pallas_call(
        kernel,
        out_shape=outs,
        in_specs=specs,
        out_specs=jax.tree.map(lambda _: vmem, outs),
        scratch_shapes=list(scratch),
        compiler_params=pltpu.CompilerParams(vmem_limit_bytes=32 * 2**20),
        cost_estimate=pl.CostEstimate(flops=gflops * 10**9, bytes_accessed=10**5, transcendentals=0),
        name=name,
    )


def shards(coords, probes, neighbours):
    count = lax.axis_size(AXES)
    quarter = probes.shape[0] // SLAB
    device = lax.axis_index(AXES)
    here = jnp.reshape(device, (1,)).astype(jnp.int32)
    smem = pl.BlockSpec(memory_space=pltpu.SMEM)
    vmem = pl.BlockSpec(memory_space=pltpu.VMEM)
    tile = jax.ShapeDtypeStruct((quarter, WIDE), F32)
    tiles = jax.ShapeDtypeStruct((SLAB, quarter, WIDE), F32)
    square = jax.ShapeDtypeStruct((PTS, WIDE), F32)

    told = jnp.pad(coords, ((0, 6), (0, 0))) + jnp.pad(
        neighbours.astype(F32), ((2, 6 - BLK), (0, WIDE - NEIGH))
    )
    told = jnp.broadcast_to(told[None], (count, 8, WIDE))
    pieces = local(prepare_kernel, "prepare", (tile,) * SLAB, [smem, vmem])(here, probes)
    own = jnp.stack([pieces[0]] + [swapped(pieces[k], k) for k in range(1, SLAB)])
    everywhere = lax.all_to_all(told, AXES, 0, 0)
    ids = lax.dynamic_slice(everywhere, (device // SLAB * SLAB, 2, 0), (SLAB, BLK, NEIGH)).astype(jnp.int32)
    early = [passed(own, SLAB * o) for o in (3, 2)]
    w, schur = local(
        factor_kernel,
        "factor",
        (jax.ShapeDtypeStruct((COND + PTS, WIDE), F32), square),
        [smem, smem, vmem],
        gflops=14,
    )(here, neighbours, everywhere)
    w, own, *early = lax.optimization_barrier((w, own, *early))
    w_y = swapped(w, 2)
    late = [passed(own, SLAB), passed(own, SPAN)]
    w_d = swapped(w, 1)
    w_y, *late = lax.optimization_barrier((w_y, *late))
    window = [own, late[0], early[1], early[0], late[1]]
    w_yd = swapped(w_y, 1)
    terms = local(
        apply_kernel,
        "apply",
        (tiles,) * WINDOW,
        [smem, smem] + [vmem] * (WINDOW + SLAB),
        [pltpu.VMEM((2 * WINDOW * SLAB, quarter, WIDE), F32)] * 2,
        gflops=4,
    )(here, ids, *window, w, w_d, w_y, w_yd)
    logs = local(
        logdet_kernel, "logdet", jax.ShapeDtypeStruct((8, WIDE), F32), [vmem], [pltpu.VMEM((PTS, WIDE), F32)], gflops=9
    )(schur)
    returned = [passed(terms[o], -SLAB * o) for o in (3, 2, 4, 1)]
    kept, logs = lax.optimization_barrier((terms[0], logs))
    sums = local(sum_kernel, "sum", (tile,) * SLAB, [vmem] * WINDOW)(kept, *returned)
    result = local(place_kernel, "place", jax.ShapeDtypeStruct(probes.shape, F32), [smem] + [vmem] * SLAB)(
        here, sums[0], *(swapped(sums[k], k) for k in range(1, SLAB))
    )
    return result, logs[0, :: PTS]


def solution(mesh):
    return jax.shard_map(
        shards,
        mesh=mesh,
        in_specs=(P(None, AXES), P(None, AXES), P(AXES, None)),
        out_specs=(P(None, AXES), P(AXES)),
        check_vma=False,
    )
```

```python
import functools

import jax
import jax.numpy as jnp
from jax import lax
from jax.experimental import pallas as pl
from jax.experimental.pallas import tpu as pltpu
from jax.sharding import PartitionSpec as P

PTS = 64
NEIGH = 8
SPAN = 16
BLK = 2
WIDE = 128
SQRT_THREE = 1.7320508075688772
NUGGET = 0.25
AXES = ("group", "shard")
SLAB = 4
WINDOW = SPAN // SLAB + 1
COND = NEIGH * PTS
STEPS = COND // WIDE
HIGHEST = lax.Precision.HIGHEST
HIGH = lax.Precision.HIGH
F32 = jnp.float32


def dot(a, b, dims=((1,), (0,)), precision=HIGHEST):
    return lax.dot_general(a, b, (dims, ((), ())), precision=precision, preferred_element_type=F32)


def quick(a, b, dims=((1,), (0,))):
    return dot(a, b, dims, HIGH)


def iota(shape, dim):
    return lax.broadcasted_iota(jnp.int32, shape, dim)


def eye(n):
    return (iota((n, n), 0) == iota((n, n), 1)).astype(F32)


def schedule(low, high):
    rho = (high - low) / (high + low)
    factors = []
    while rho > 3e-4:
        factors.append(2.0 / (2.0 - rho * rho))
        rho = rho * rho / (2.0 - rho * rho)
    return 2.0 / (low + high), factors


def split(a):
    high = a.astype(jnp.bfloat16)
    return high, (a - high.astype(F32)).astype(jnp.bfloat16)


def products(lefts, right):
    high, low = split(right)
    rows = [jnp.concatenate([h, low_part, h], axis=1) for h, low_part in map(split, lefts)]
    out = lax.dot_general(
        jnp.concatenate(rows, axis=0),
        jnp.concatenate([high, high, low], axis=0),
        (((1,), (0,)), ((), ())),
        preferred_element_type=F32,
    )
    n = right.shape[0]
    return [out[i * n : (i + 1) * n] for i in range(len(lefts))]


def inverses(mats, top, tasks):
    alpha, factors = schedule(0.245, top + 0.26)
    stages = len(factors) + 1

    def spread(stage):
        for task in tasks[stage * len(tasks) // stages : (stage + 1) * len(tasks) // stages]:
            task()

    ident = eye(WIDE)
    rs = [ident - alpha * m for m in mats]
    c = factors[0]
    xs = [(alpha * c) * (ident + r) for r in rs]
    rs = [(1.0 - c) * ident + c * products([r], r)[0] for r in rs]
    spread(0)
    for stage, c in enumerate(factors[1:-1]):
        pairs = [products([x, r], r) for x, r in zip(xs, rs)]
        xs = [c * (x + xr) for x, (xr, _) in zip(xs, pairs)]
        rs = [(1.0 - c) * ident + c * rr for _, rr in pairs]
        spread(stage + 1)
    c = factors[-1]
    xs = [c * (x + products([x], r)[0]) for x, r in zip(xs, rs)]
    spread(stages - 2)
    es = [ident - dot(m, x) for m, x in zip(mats, xs)]
    spread(stages - 1)
    return [x + products([x], e)[0] for x, e in zip(xs, es)]


def kernel_value(dx, dy):
    s = SQRT_THREE * jnp.sqrt(dx * dx + dy * dy)
    return (1.0 + s) * jnp.exp(-s)


def place_of(me, device):
    return (lax.div(me, SLAB) - lax.div(device, SLAB)) * SLAB + (lax.rem(device, SLAB) ^ lax.rem(me, SLAB))


def factor_kernel(where_ref, nb_ref, coords_ref, g_ref, s_ref):
    me = where_ref[0]
    lane = iota((1, WIDE), 1)
    low = lane < PTS

    def half_row(dev, half, coord, to_low):
        row = coords_ref[dev, pl.ds(coord, 1), :]
        swapped = pltpu.roll(row, PTS, 1)
        take = half if to_low else 1 - half
        return jnp.where(take == 1, swapped, row)

    def column(row):
        return jnp.transpose(jnp.broadcast_to(row, (WIDE, WIDE)))

    points = []
    for b in range(BLK):
        rows, valid = [], []
        for k in range(STEPS):
            pieces, oks = [], []
            for h in range(2):
                ident = nb_ref[b, 2 * k + h]
                ok = ident >= 0
                safe = jnp.where(ok, ident, me * BLK)
                dev, half = lax.div(safe, BLK), lax.rem(safe, BLK)
                pieces.append([half_row(dev, half, c, h == 0) for c in range(2)])
                oks.append(jnp.where(ok, 1.0, 0.0).astype(F32))
            rows.append([jnp.where(low, pieces[0][c], pieces[1][c]) for c in range(2)])
            valid.append(jnp.where(low, oks[0], oks[1]))
        own = [half_row(me, b, c, True) for c in range(2)]
        cols = [[column(r) for r in row] for row in rows]
        own_cols = [column(r)[:PTS, :PTS] for r in own]
        valid_cols = [column(v) for v in valid]
        points.append((rows, valid, own, cols, own_cols, valid_cols))

    mats = [{} for _ in range(BLK)]
    panels = [{} for _ in range(BLK)]
    solved = [{} for _ in range(BLK)]

    def covariance(b, i, j):
        rows, valid, own, cols, own_cols, valid_cols = points[b]
        if i == STEPS:
            value = kernel_value(own_cols[0] - own[0][:, :PTS], own_cols[1] - own[1][:, :PTS])
            value = value + NUGGET * eye(PTS)
        elif j == STEPS:
            value = kernel_value(cols[i][0][:, :PTS] - own[0][:, :PTS], cols[i][1][:, :PTS] - own[1][:, :PTS])
            value = valid_cols[i][:, :PTS] * value
        else:
            value = kernel_value(cols[i][0] - rows[j][0], cols[i][1] - rows[j][1])
            value = valid_cols[i] * valid[j] * value
            if i == j:
                value = value + eye(WIDE) * (NUGGET * valid[j] + (1.0 - valid[j]))
        mats[b][i, j] = value

    def panel(b, k, j, inv):
        panels[b][k, j] = dot(inv, mats[b][k, j])

    def update(b, k, i, j):
        mats[b][i, j] = mats[b][i, j] - dot(mats[b][k, i], panels[b][k, j], ((0,), (0,)))

    def substitute(b, k):
        total = panels[b][k, STEPS]
        for j in range(k + 1, STEPS):
            total = total - dot(panels[b][k, j], solved[b][j])
        solved[b][k] = total

    def store(k):
        g_ref[k * WIDE : (k + 1) * WIDE, :] = -jnp.concatenate([s[k] for s in solved], axis=1)

    blocks = range(BLK)
    for i in range(STEPS + 1):
        for j in range(i, STEPS + 1):
            for b in blocks:
                covariance(b, i, j)
    tasks = []
    for k in range(STEPS):
        invs = inverses([m[k, k] for m in mats], WIDE, tasks)
        for b in blocks:
            panel(b, k, k + 1, invs[b])
        for b in blocks:
            update(b, k, k + 1, k + 1)
        tasks = [functools.partial(panel, b, k, j, invs[b]) for j in range(k + 2, STEPS + 1) for b in blocks]
        tasks += [
            functools.partial(update, b, k, i, j)
            for i in range(k + 1, STEPS + 1)
            for j in range(i, STEPS + 1)
            for b in blocks
            if (i, j) != (k + 1, k + 1)
        ]
    for k in reversed(range(STEPS)):
        tasks += [functools.partial(substitute, b, k) for b in blocks] + [functools.partial(store, k)]
    schur = [m[STEPS, STEPS] for m in mats]
    gap = jnp.zeros((PTS, PTS), F32)
    both = jnp.concatenate(
        [jnp.concatenate([schur[0], gap], axis=1), jnp.concatenate([gap, schur[1]], axis=1)], axis=0
    )
    both = inverses([both], PTS, tasks)[0]
    g_ref[COND:, :] = jnp.where(low, both[:PTS], both[PTS:])
    s_ref[...] = jnp.concatenate(schur, axis=1)


def apply_kernel(where_ref, ids_ref, *rest):
    windows, w_refs, outs = rest[:WINDOW], rest[WINDOW : WINDOW + SLAB], rest[WINDOW + SLAB : -2]
    held, total = rest[-2], rest[-1]
    me = where_ref[0]
    slab, quarter = lax.div(me, SLAB), lax.rem(me, SLAB)
    low = iota((PTS, WIDE), 1) < PTS
    places_held = WINDOW * SLAB
    for o in range(WINDOW):
        for q in range(SLAB):
            tile = windows[o][q]
            held[o * SLAB + q] = tile
            held[places_held + o * SLAB + q] = pltpu.roll(tile, PTS, 1)
    total[...] = jnp.zeros_like(total)

    places = []
    for k in range(SLAB):
        device = slab * SLAB + (quarter ^ k)
        for b in range(BLK):
            for m in range(NEIGH):
                ident = ids_ref[quarter ^ k, b, m]
                ident = jnp.where(ident >= 0, ident, device * BLK)
                turned = lax.rem(ident, BLK) ^ (m % 2)
                places.append(place_of(me, lax.div(ident, BLK)) + turned * places_held)
    gathered = []
    for k in range(SLAB):
        sides = []
        for b in range(BLK):
            at = places[(k * BLK + b) * NEIGH : (k * BLK + b + 1) * NEIGH]
            pieces = [jnp.where(low, held[at[m]], held[at[m + 1]]) for m in range(0, NEIGH, 2)]
            sides.append(jnp.concatenate(pieces, axis=1))
        gathered.append(jnp.concatenate(sides, axis=0))
    whites = [quick(gathered[k], w_refs[k][:COND, :]) for k in range(SLAB)]
    scaled = []
    for k in range(SLAB):
        white = held[k] + jnp.where(low, whites[k][:PTS], whites[k][PTS:])
        v = w_refs[k][COND:, :]
        inv = jnp.concatenate([jnp.where(low, v, 0.0), jnp.where(low, 0.0, v)], axis=0)
        scaled.append(dot(white, inv))
    backs = []
    for k in range(SLAB):
        sides = jnp.concatenate([jnp.where(low, scaled[k], 0.0), jnp.where(low, 0.0, scaled[k])], axis=0)
        backs.append(quick(sides, w_refs[k][:COND, :], ((1,), (1,))))
    for k in range(SLAB):
        total[k] = scaled[k]
    for k in range(SLAB):
        for b in range(BLK):
            for m in range(NEIGH):
                tile = backs[k][b * PTS : (b + 1) * PTS, (m // 2) * WIDE : (m // 2 + 1) * WIDE]
                tile = jnp.where(low, tile, 0.0) if m % 2 == 0 else jnp.where(low, 0.0, tile)
                total[places[(k * BLK + b) * NEIGH + m]] += tile
    for o in range(WINDOW):
        for q in range(SLAB):
            place = o * SLAB + q
            outs[o][q] = total[place] + pltpu.roll(total[places_held + place], PTS, 1)


def logdet_kernel(s_ref, out_ref, work):
    work[...] = s_ref[...]
    rows = iota((PTS, WIDE), 0)
    lanes = iota((PTS, WIDE), 1)

    def step(k, total):
        mat = work[...]
        row = work[pl.ds(k, 1), :]
        first = jnp.sum(jnp.where(lanes == k, mat, 0.0), axis=1, keepdims=True)
        second = jnp.sum(jnp.where(lanes == k + PTS, mat, 0.0), axis=1, keepdims=True)
        col = jnp.where(lanes < PTS, first, second)
        pivot = jnp.sum(jnp.where(rows == k, col, 0.0), axis=0, keepdims=True)
        work[...] = mat - col * (row / pivot)
        return total + jnp.log(pivot)

    total = lax.fori_loop(0, PTS, step, jnp.zeros((1, WIDE), F32))
    out_ref[...] = jnp.broadcast_to(total * (1.0 / PTS), out_ref.shape)


def prepare_kernel(where_ref, probes_ref, *outs):
    quarter = lax.rem(where_ref[0], SLAB)
    rows = outs[0].shape[0]
    for k in range(SLAB):
        outs[k][...] = probes_ref[pl.ds(pl.multiple_of((quarter ^ k) * rows, rows), rows), :]


def sum_kernel(*refs):
    terms, outs = refs[:WINDOW], refs[WINDOW:]
    for k in range(SLAB):
        value = terms[0][k]
        for o in range(1, WINDOW):
            value = value + terms[o][k]
        outs[k][...] = value


def place_kernel(where_ref, *refs):
    tiles, out_ref = refs[:SLAB], refs[SLAB]
    quarter = lax.rem(where_ref[0], SLAB)
    rows = tiles[0].shape[0]
    for k in range(SLAB):
        out_ref[pl.ds(pl.multiple_of((quarter ^ k) * rows, rows), rows), :] = tiles[k][...]


def passed(value, by):
    size = lax.axis_size(AXES)
    return lax.ppermute(value, AXES, [(i, i + by) for i in range(size) if 0 <= i + by < size])


def swapped(value, mask):
    size = lax.axis_size(AXES)
    return lax.ppermute(value, AXES, [(i, i ^ mask) for i in range(size)])


def local(kernel, name, outs, specs, scratch=(), gflops=1):
    vmem = pl.BlockSpec(memory_space=pltpu.VMEM)
    return pl.pallas_call(
        kernel,
        out_shape=outs,
        in_specs=specs,
        out_specs=jax.tree.map(lambda _: vmem, outs),
        scratch_shapes=list(scratch),
        compiler_params=pltpu.CompilerParams(vmem_limit_bytes=32 * 2**20),
        cost_estimate=pl.CostEstimate(flops=gflops * 10**9, bytes_accessed=10**5, transcendentals=0),
        name=name,
    )


def shards(coords, probes, neighbours):
    count = lax.axis_size(AXES)
    quarter = probes.shape[0] // SLAB
    device = lax.axis_index(AXES)
    here = jnp.reshape(device, (1,)).astype(jnp.int32)
    smem = pl.BlockSpec(memory_space=pltpu.SMEM)
    vmem = pl.BlockSpec(memory_space=pltpu.VMEM)
    tile = jax.ShapeDtypeStruct((quarter, WIDE), F32)
    tiles = jax.ShapeDtypeStruct((SLAB, quarter, WIDE), F32)
    square = jax.ShapeDtypeStruct((PTS, WIDE), F32)

    told = jnp.pad(coords, ((0, BLK), (0, 0))) + jnp.pad(
        neighbours.astype(F32), ((2, 0), (0, WIDE - NEIGH))
    )
    told = jnp.broadcast_to(told[None], (count, 2 + BLK, WIDE))
    pieces = local(prepare_kernel, "prepare", (tile,) * SLAB, [smem, vmem])(here, probes)
    own = jnp.stack([pieces[0]] + [swapped(pieces[k], k) for k in range(1, SLAB)])
    everywhere = lax.all_to_all(told, AXES, 0, 0)
    ids = lax.dynamic_slice(everywhere, (device // SLAB * SLAB, 2, 0), (SLAB, BLK, NEIGH)).astype(jnp.int32)
    early = [passed(own, SLAB * o) for o in (3, 2)]
    w, schur = local(
        factor_kernel,
        "factor",
        (jax.ShapeDtypeStruct((COND + PTS, WIDE), F32), square),
        [smem, smem, vmem],
        gflops=14,
    )(here, neighbours, everywhere)
    w, own, *early = lax.optimization_barrier((w, own, *early))
    w_y = swapped(w, 2)
    late = [passed(own, SLAB), passed(own, SPAN)]
    w_d = swapped(w, 1)
    w_y, *late = lax.optimization_barrier((w_y, *late))
    window = [own, late[0], early[1], early[0], late[1]]
    w_yd = swapped(w_y, 1)
    terms = local(
        apply_kernel,
        "apply",
        (tiles,) * WINDOW,
        [smem, smem] + [vmem] * (WINDOW + SLAB),
        [pltpu.VMEM((2 * WINDOW * SLAB, quarter, WIDE), F32)] * 2,
        gflops=4,
    )(here, ids, *window, w, w_d, w_y, w_yd)
    logs = local(
        logdet_kernel, "logdet", jax.ShapeDtypeStruct((8, WIDE), F32), [vmem], [pltpu.VMEM((PTS, WIDE), F32)], gflops=9
    )(schur)
    returned = [passed(terms[o], -SLAB * o) for o in (3, 2, 4, 1)]
    kept, logs = lax.optimization_barrier((terms[0], logs))
    sums = local(sum_kernel, "sum", (tile,) * SLAB, [vmem] * WINDOW)(kept, *returned)
    result = local(place_kernel, "place", jax.ShapeDtypeStruct(probes.shape, F32), [smem] + [vmem] * SLAB)(
        here, sums[0], *(swapped(sums[k], k) for k in range(1, SLAB))
    )
    return result, logs[0, :: PTS]


def solution(mesh):
    return jax.shard_map(
        shards,
        mesh=mesh,
        in_specs=(P(None, AXES), P(None, AXES), P(AXES, None)),
        out_specs=(P(None, AXES), P(AXES)),
        check_vma=False,
    )
```
